32 devices in a mesh: seq: 8 (over z, y), chan: 4 (over x, core).
Axes of the slice: x: 2, y: 2, z: 4, core: 2. Of those that a mesh axis runs over, the one named last changes fastest.
Arguments:
- tokens: bfloat16 [4096, 8192], P('seq', 'chan'), may hold values from -6 to 6
- norm_gain: float32 [8192], replicated, may hold values from 0.1 to 1.9
- w_in: bfloat16 [8192, 3, 4096], P('seq', None, 'chan'), may hold values from -0.0625 to 0.0625
- short_taps: float32 [3, 3, 4096], P(None, None, 'chan'), may hold values from -3.6 to 3.6
- medium_taps: float32 [128, 256], P(None, 'chan'), may hold values from -0.75 to 0.75
- skip_gain: float32 [4096], P('chan'), may hold values from 0.5 to 1.5
- w_out: bfloat16 [4096, 8192], P('chan'), may hold values from -0.09375 to 0.09375
Outputs:
- block_out: bfloat16 [4096, 8192], P('seq', 'chan')
The draws below stay inside these ranges and needn't reach their ends.
All inputs are finite; a program needn't handle non-finite values.
Results may differ from the reference program's by a relative error of at most 0.019.
Values may be sent and summed in bfloat16 or wider, within the bound.
No kernel may reach another device: no remote copies, remote signals or barrier semaphores. Data moves between devices by JAX's collectives and lax.ppermute only.
A program may use at most 192 MiB of HBM per device.

```python
import math
import jax
import jax.numpy as jnp
from jax import lax

D = 8192
HC = 4096
TAPS = 128
GROUP = 16
TOKENS = 4096
FILT = 256
N_CHAN = 4


def draw_medium_taps(key, part):
    rate_key, base_key = jax.random.split(key)
    tap_position = jnp.arange(TAPS, dtype=jnp.float32)[:, None]
    decay_rate = jnp.exp(jax.random.uniform(rate_key, (1, FILT), jnp.float32, math.log(1.0 / 512.0), math.log(1.0 / 12.0)))
    values = jnp.clip(jax.random.normal(base_key, (TAPS, FILT), jnp.float32), -6.0, 6.0)
    return 0.12 * values * jnp.exp(-decay_rate * tap_position)


def block_levels(key, shape, pieces, low, high):
    def one(position, parts):
        heights = jax.random.uniform(jax.random.fold_in(jax.random.fold_in(key, 6), position), (parts,), jnp.float32, low / len(pieces), high / len(pieces))
        return jnp.repeat(jnp.exp(heights), shape[position] // parts).reshape((-1,) + (1,) * (len(shape) - position - 1))

    factor_of = one(*pieces[0])
    for cut in pieces[1:]:
        factor_of = factor_of * one(*cut)
    return factor_of


def gaussian(stream_key, dims, width, most, cuts=(), kind=jnp.bfloat16):
    drawn = width * jax.random.normal(stream_key, dims, jnp.float32)
    if cuts:
        drawn = drawn * block_levels(stream_key, dims, cuts, -0.22, 0.18)
    return jnp.clip(drawn, -most, most).astype(kind)


def setup_inputs(seed: int = 0) -> dict:
    key_of = jax.random.split(jax.random.key(seed), 8)
    tokens = gaussian(key_of[0], (TOKENS, D), 1.0, 6.0, ((0, 8), (1, 4)))
    norm_gain = jnp.clip(1.0 + 0.18 * jax.random.normal(key_of[1], (D,), jnp.float32), 0.1, 1.9)
    w_in = gaussian(key_of[2], (D, 3, HC), D ** -0.5, 0.0625, ((0, 8), (2, 4)))
    short_taps = gaussian(key_of[3], (3, 3, HC), 0.6, 3.6, ((2, 4),), jnp.float32)
    medium_taps = draw_medium_taps(jax.random.fold_in(key_of[7], 71), 0)
    skip_gain = jnp.clip(0.5 + 1.0 * jax.random.uniform(key_of[5], (HC,), jnp.float32) ** block_levels(key_of[5], (HC,), ((0, 4),), -0.2, 0.2), 0.5, 1.5)
    w_out = gaussian(key_of[6], (HC, D), HC ** -0.5, 0.09375, ((0, 4),))
    return {"tokens": tokens, "norm_gain": norm_gain, "w_in": w_in, "short_taps": short_taps, "medium_taps": medium_taps, "skip_gain": skip_gain, "w_out": w_out}


EPSILON = 1e-06

def delayed(values, lag_rows):
    padding = jnp.zeros((lag_rows,) + values.shape[1:], values.dtype)
    return jnp.concatenate([padding, values[:values.shape[0] - lag_rows]], 0)

def reference(tokens, norm_gain, w_in, short_taps, medium_taps, skip_gain, w_out):
    widened = tokens.astype(jnp.float32)
    mean_square = lax.optimization_barrier(jnp.mean(widened * widened, axis=1, keepdims=True))
    normed = (widened * lax.rsqrt(mean_square + EPSILON) * norm_gain).astype(jnp.bfloat16)
    projected = jnp.dot(normed, w_in.reshape(D, 3 * HC), preferred_element_type=jnp.float32)
    projected = lax.optimization_barrier(projected.astype(jnp.bfloat16))
    projected = projected.reshape(TOKENS, 3, HC).astype(jnp.float32)
    filtered = short_taps[0] * projected + short_taps[1] * delayed(projected, 1) + short_taps[2] * delayed(projected, 2)
    product = lax.optimization_barrier((filtered[:, 1] * filtered[:, 2]).astype(jnp.bfloat16)).astype(jnp.float32)
    per_channel = jnp.repeat(medium_taps, GROUP, axis=1)
    padded = jnp.concatenate([jnp.zeros((TAPS - 1, HC), jnp.float32), product], 0)

    def add_tap(tap_index, running):
        offset = (TAPS - 1 - tap_index).astype(jnp.int32)
        window = lax.dynamic_slice_in_dim(padded, offset, TOKENS, 0)
        weights = lax.dynamic_index_in_dim(per_channel, tap_index.astype(jnp.int32), 0, keepdims=False)
        return running + weights * window
    mixing = lax.fori_loop(0, TAPS, add_tap, skip_gain * product)
    gating = (filtered[:, 0] * mixing).astype(jnp.bfloat16)
    shard_width = HC // N_CHAN

    def add_shard(running, shard_index):
        start = (shard_index * shard_width).astype(jnp.int32)
        columns = lax.dynamic_slice_in_dim(gating, start, shard_width, 1)
        rows = lax.dynamic_slice_in_dim(w_out, start, shard_width, 0)
        partial_sum = jnp.dot(columns, rows, preferred_element_type=jnp.float32)
        rounded = lax.optimization_barrier(partial_sum.astype(jnp.bfloat16)).astype(jnp.float32)
        return (running + rounded, None)
    summed, _ = lax.scan(add_shard, jnp.zeros((TOKENS, D), jnp.float32), jnp.arange(N_CHAN, dtype=jnp.int32))
    output = widened + summed
    return output.astype(jnp.bfloat16)
```

```python
import jax
import jax.numpy as jnp
from jax import lax
from jax.sharding import PartitionSpec as P

TAPS = 128
GROUP = 16
PIECES = 4
EPSILON = 1e-06


def passed_along(value, axis, steps):
    count = lax.axis_size(axis)
    first, last = (max(0, -steps), min(count, count - steps))
    return lax.ppermute(value, axis, [(source, source + steps) for source in range(first, last)])


def swapped(value, axis, bit):
    return lax.ppermute(value, axis, [(i, i ^ bit) for i in range(lax.axis_size(axis))])


def short_filter(extended, taps):
    return taps[0] * extended[2:] + taps[1] * extended[1:-1] + taps[2] * extended[:-2]


def spread_tokens(tokens, norm_gain):
    seq, chan = lax.axis_size("seq"), lax.axis_size("chan")
    layers = seq // 2
    groups = [list(range(start, seq, 2)) for start in range(2)]
    odd = lax.axis_index("seq") % 2 == 1
    whole = lax.all_to_all(tokens, "chan", 0, 1, tiled=True)
    widened = whole.astype(jnp.float32)
    mean_square = jnp.mean(widened * widened, axis=1, keepdims=True)
    normed = (widened * lax.rsqrt(mean_square + EPSILON) * norm_gain).astype(jnp.bfloat16)
    rows, depth = normed.shape
    halves = normed.reshape(rows, layers, 2, depth // seq)
    halves = jnp.where(odd, halves[:, :, ::-1], halves).reshape(rows, depth)
    shared = lax.all_to_all(halves, "seq", 1, 0, axis_index_groups=groups, tiled=True)
    shared = shared.reshape(layers, rows, depth // layers)
    return lax.all_gather(shared, "chan", axis=1, tiled=True)


def toeplitz_of(medium_taps):
    cube_shape = (TAPS, TAPS, 2 * TAPS)
    lagged = (
        lax.broadcasted_iota(jnp.int32, cube_shape, 1)
        + TAPS
        - lax.broadcasted_iota(jnp.int32, cube_shape, 2)
    )
    onehot = (lagged == lax.broadcasted_iota(jnp.int32, cube_shape, 0)).astype(jnp.bfloat16)
    return jnp.einsum("jg,jis->gis", medium_taps.astype(jnp.bfloat16), onehot)


def mixed(projected, short_taps, toeplitz, skip_gain):
    row_count, _, channels = projected.shape
    edge_rows = passed_along(projected[row_count - 2 :], "seq", 1)
    extended = jnp.concatenate([edge_rows, projected], 0).astype(jnp.float32)
    filtered = short_filter(extended, short_taps)
    queries = filtered[:, 0]
    product = (filtered[:, 1] * filtered[:, 2]).astype(jnp.bfloat16)
    product_rows = passed_along(product[row_count - TAPS :], "seq", 1)
    padded = jnp.concatenate([product_rows, product], 0)
    block_count = row_count // TAPS
    blocks = padded.reshape(block_count + 1, TAPS, channels)
    windows = jnp.concatenate([blocks[:-1], blocks[1:]], 1)
    filters = channels // GROUP
    grouped = windows.reshape(block_count, 2 * TAPS, filters, GROUP)
    convolved = jnp.einsum("gis,bsgc->bigc", toeplitz, grouped, preferred_element_type=jnp.float32)
    mixing = skip_gain * product.astype(jnp.float32) + convolved.reshape(row_count, channels)
    return (queries * mixing).astype(jnp.bfloat16)


def per_device(tokens, norm_gain, w_in, short_taps, medium_taps, skip_gain, w_out):
    seq, chan = lax.axis_size("seq"), lax.axis_size("chan")
    layers = seq // 2
    groups = [list(range(start, seq, 2)) for start in range(2)]
    row_count = tokens.shape[0]
    channels = w_in.shape[2]
    width = channels // PIECES
    pieces = [w_in[:, :, i * width : (i + 1) * width] for i in range(PIECES)]
    pieces = [piece.reshape(piece.shape[0], 3 * width) for piece in pieces]
    others = [swapped(piece, "seq", 1) for piece in pieces]
    spread = spread_tokens(tokens, norm_gain)
    spread = spread.reshape(layers * row_count, spread.shape[2])
    toeplitz = toeplitz_of(medium_taps)
    filters = width // GROUP
    gates = []
    for i in range(PIECES):
        section = jnp.concatenate([pieces[i], others[i]], 0)
        summed = jnp.dot(spread, section, preferred_element_type=jnp.float32).astype(jnp.bfloat16)
        projected = lax.psum_scatter(
            summed, "seq", scatter_dimension=0, axis_index_groups=groups, tiled=True
        )
        span = slice(i * width, (i + 1) * width)
        gates.append(
            mixed(
                projected.reshape(row_count, 3, width),
                short_taps[:, :, span],
                toeplitz[i * filters : (i + 1) * filters],
                skip_gain[span],
            )
        )
    gating = jnp.concatenate(gates, 1)
    partial_out = jnp.dot(gating, w_out, preferred_element_type=jnp.float32).astype(jnp.bfloat16)
    projected_out = lax.psum_scatter(partial_out, "chan", scatter_dimension=1, tiled=True)
    return (tokens.astype(jnp.float32) + projected_out.astype(jnp.float32)).astype(jnp.bfloat16)


def solution(mesh):
    in_specs = (
        P("seq", "chan"),
        P(),
        P("seq", None, "chan"),
        P(None, None, "chan"),
        P(None, "chan"),
        P("chan"),
        P("chan", None),
    )
    out_specs = P("seq", "chan")
    return jax.shard_map(
        per_device, mesh=mesh, in_specs=in_specs, out_specs=out_specs, check_vma=False
    )
```

```python
import jax
import jax.numpy as jnp
from jax import lax
from jax.experimental import pallas as pl
from jax.experimental.pallas import tpu as pltpu
from jax.sharding import PartitionSpec as P

TAPS = 128
GROUP = 16
EDGE = TAPS + 16
PARTS = 2
EPSILON = 1e-06


def swapped(value, axis, bit):
    return lax.ppermute(value, axis, [(i, i ^ bit) for i in range(lax.axis_size(axis))])


def project(order, rows, sections, addend):
    count, depth = rows.shape
    step, width = sections[0].shape
    tile = min(count, 256)

    def kernel(order_ref, rows_ref, *refs):
        total = jnp.zeros((tile, width), jnp.float32)
        for i in range(len(sections)):
            place = pl.ds(pl.multiple_of(order_ref[i] * step, step), step)
            total += jnp.dot(rows_ref[:, place], refs[i][...], preferred_element_type=jnp.float32)
        if addend is not None:
            total += refs[len(sections)][...].astype(jnp.float32)
        refs[-1][...] = total.astype(jnp.bfloat16)

    whole = pl.BlockSpec((step, width), lambda i, _: (0, 0))
    piece = pl.BlockSpec((tile, width), lambda i, _: (i, 0))
    extra = [] if addend is None else [addend]
    return pl.pallas_call(
        kernel,
        grid_spec=pltpu.PrefetchScalarGridSpec(
            num_scalar_prefetch=1,
            grid=(count // tile,),
            in_specs=[pl.BlockSpec((tile, depth), lambda i, _: (i, 0))]
            + [whole] * len(sections)
            + [piece] * len(extra),
            out_specs=piece,
        ),
        out_shape=jax.ShapeDtypeStruct((count, width), jnp.bfloat16),
        compiler_params=pltpu.CompilerParams(vmem_limit_bytes=40 << 20),
        cost_estimate=pl.CostEstimate(
            flops=2 * count * depth * width,
            bytes_accessed=2 * (count * depth + depth * width + count * width),
            transcendentals=0,
        ),
        name="project",
    )(order, rows, *sections, *extra)


def gate(halo, parts, short_taps, skip_gain, toeplitz):
    slots, part_rows, wide = parts[0].shape
    width = wide // 3
    row_count = part_rows * len(parts)
    filters = toeplitz.shape[1] // (2 * TAPS)

    def kernel(halo_ref, *refs):
        part_refs = refs[: len(parts)]
        taps_ref, skip_ref, toeplitz_ref, out_ref, extended = refs[len(parts) :]
        extended[:EDGE] = halo_ref[0].astype(jnp.float32)
        for i, ref in enumerate(part_refs):
            extended[EDGE + i * part_rows : EDGE + (i + 1) * part_rows] = ref[0].astype(jnp.float32)
        rows = TAPS + row_count
        filtered = sum(
            taps_ref[lag : lag + 1] * extended[16 - lag : 16 - lag + rows] for lag in range(3)
        )
        product = filtered[:, width : 2 * width] * filtered[:, 2 * width :]
        product = product.astype(jnp.bfloat16)
        owner = lax.broadcasted_iota(jnp.int32, (2 * TAPS, width), 1) // GROUP
        for start in range(0, row_count, TAPS):
            window = product[start : start + 2 * TAPS]
            spread = jnp.concatenate(
                [jnp.where(owner == f, window, jnp.zeros_like(window)) for f in range(filters)], 0
            )
            convolved = jnp.dot(toeplitz_ref[...], spread, preferred_element_type=jnp.float32)
            mixing = skip_ref[...] * window[TAPS:].astype(jnp.float32) + convolved
            queries = filtered[TAPS + start : 2 * TAPS + start, :width]
            out_ref[0, start : start + TAPS] = (queries * mixing).astype(jnp.bfloat16)

    slot = lambda i: (i, 0, 0)
    fixed = lambda i: (0, 0)
    return pl.pallas_call(
        kernel,
        grid=(slots,),
        in_specs=[pl.BlockSpec((1, EDGE, wide), slot)]
        + [pl.BlockSpec((1, part_rows, wide), slot)] * len(parts)
        + [
            pl.BlockSpec((3, wide), fixed),
            pl.BlockSpec((1, width), fixed),
            pl.BlockSpec((TAPS, 2 * TAPS * filters), fixed),
        ],
        out_specs=pl.BlockSpec((1, row_count, width), slot),
        out_shape=jax.ShapeDtypeStruct((slots, row_count, width), jnp.bfloat16),
        scratch_shapes=[pltpu.VMEM((EDGE + row_count, wide), jnp.float32)],
        compiler_params=pltpu.CompilerParams(vmem_limit_bytes=40 << 20),
        cost_estimate=pl.CostEstimate(
            flops=2 * slots * row_count * 2 * TAPS * filters * width,
            bytes_accessed=2 * slots * row_count * 4 * width,
            transcendentals=0,
        ),
        name="gate",
    )(halo, *parts, short_taps, skip_gain, toeplitz)


def out_block(gating, w_out, block, count):
    rows, depth = gating.shape
    columns = w_out.shape[1] // count
    tile = min(columns, 512)
    steps = columns // tile

    def kernel(block_ref, gating_ref, w_ref, out_ref):
        out_ref[...] = jnp.dot(
            gating_ref[...], w_ref[...], preferred_element_type=jnp.float32
        ).astype(jnp.bfloat16)

    return pl.pallas_call(
        kernel,
        grid_spec=pltpu.PrefetchScalarGridSpec(
            num_scalar_prefetch=1,
            grid=(steps,),
            in_specs=[
                pl.BlockSpec((rows, depth), lambda i, b: (0, 0)),
                pl.BlockSpec((depth, tile), lambda i, b: (0, b[0] * steps + i)),
            ],
            out_specs=pl.BlockSpec((rows, tile), lambda i, b: (0, i)),
        ),
        out_shape=jax.ShapeDtypeStruct((rows, columns), jnp.bfloat16),
        compiler_params=pltpu.CompilerParams(vmem_limit_bytes=40 << 20),
        cost_estimate=pl.CostEstimate(
            flops=2 * rows * depth * columns,
            bytes_accessed=2 * (rows * depth + depth * columns + rows * columns),
            transcendentals=0,
        ),
        name="out_block",
    )(block.reshape(1).astype(jnp.int32), gating, w_out)


def toeplitz_of(medium_taps):
    cube_shape = (TAPS, TAPS, 2 * TAPS)
    lagged = (
        lax.broadcasted_iota(jnp.int32, cube_shape, 1)
        + TAPS
        - lax.broadcasted_iota(jnp.int32, cube_shape, 2)
    )
    onehot = (lagged == lax.broadcasted_iota(jnp.int32, cube_shape, 0)).astype(jnp.bfloat16)
    return jnp.einsum("jg,jis->igs", medium_taps.astype(jnp.bfloat16), onehot)


def per_device(tokens, norm_gain, w_in, short_taps, medium_taps, skip_gain, w_out):
    seq, chan = lax.axis_size("seq"), lax.axis_size("chan")
    here, column = lax.axis_index("seq"), lax.axis_index("chan")
    near = seq // 4
    odd, layer = here % 2, here // 2
    half, place = layer // near, layer % near
    row_count = tokens.shape[0]
    depth = norm_gain.shape[0]
    channels = w_in.shape[2]
    mine = channels // near
    pieces = max(1, mine // 128)
    width = mine // pieces
    part_rows = row_count // PARTS

    order = jnp.stack([(place ^ o) * 2 + (odd ^ p) for o in range(near) for p in range(2)])
    order = order.astype(jnp.int32)
    sections = []
    for i in range(pieces):
        held = []
        for o in range(near):
            start = (place ^ o) * mine + i * width
            cut = lax.dynamic_slice_in_dim(w_in, start, width, 2).reshape(w_in.shape[0], 3 * width)
            held.append(cut if o == 0 else swapped(cut, "seq", 2 * o))
        both = []
        for cut in held:
            both += [cut, swapped(cut, "seq", 1)]
        sections.append(both)

    away_rows, own_rows = [], []
    for i in range(PARTS):
        part = tokens[i * part_rows : (i + 1) * part_rows]
        widened = lax.all_to_all(part, "chan", 0, 1, tiled=True).astype(jnp.float32)
        mean_square = jnp.mean(widened * widened, axis=1, keepdims=True)
        normed = (widened * lax.rsqrt(mean_square + EPSILON) * norm_gain).astype(jnp.bfloat16)
        keep = lax.dynamic_slice_in_dim(normed, half * (depth // 2), depth // 2, 1)
        send = lax.dynamic_slice_in_dim(normed, (1 - half) * (depth // 2), depth // 2, 1)
        for rows, kept in ((swapped(send, "seq", 2 * near), away_rows), (keep, own_rows)):
            layers = [rows if o == 0 else swapped(rows, "seq", 2 * o) for o in range(near)]
            rows = lax.all_gather(jnp.stack(layers), "chan", axis=1, tiled=True)
            kept.append(rows.reshape(near * part_rows, depth // 2))

    short = lax.dynamic_slice_in_dim(short_taps, place * mine, mine, 2)
    skip = lax.dynamic_slice_in_dim(skip_gain, place * mine, mine, 0).reshape(1, mine)
    filters = medium_taps.shape[1] // near
    toeplitz = toeplitz_of(lax.dynamic_slice_in_dim(medium_taps, place * filters, filters, 1))
    some = filters // pieces
    far = [(2 * i + 1, 2 * (near + i)) for i in range(near)]
    gates = []
    for i in range(pieces):
        sums = []
        for j in range(PARTS):
            sent = project(order, away_rows[j], sections[i], None)
            sums.append(swapped(sent, "seq", 2 * near))
        sums = [
            project(order, own_rows[j], sections[i], sums[j]).reshape(near, part_rows, 3 * width)
            for j in range(PARTS)
        ]
        edge = sums[-1][:, part_rows - EDGE :]
        edge = jnp.stack([lax.dynamic_index_in_dim(edge, place ^ o, 0, False) for o in range(near)])
        across = swapped(edge, "seq", 1)
        before = jnp.concatenate([lax.ppermute(edge[-1:], "seq", far), across[:-1]], 0)
        halo = jnp.where(odd == 1, across, before)
        halo = jnp.stack([lax.dynamic_index_in_dim(halo, place ^ o, 0, False) for o in range(near)])
        span = slice(i * width, (i + 1) * width)
        gated = gate(
            halo,
            sums,
            short[:, :, span].reshape(3, 3 * width),
            skip[:, span],
            toeplitz[:, i * some : (i + 1) * some].reshape(TAPS, some * 2 * TAPS),
        )
        gates.append([gated[0]] + [swapped(gated[o], "seq", 2 * o) for o in range(1, near)])
    gating = jnp.zeros((row_count, channels), jnp.bfloat16)
    for o in range(near):
        share = jnp.concatenate([piece[o] for piece in gates], 1)
        gating = lax.dynamic_update_slice(gating, share, (0, (place ^ o) * mine))

    total = tokens.astype(jnp.float32)
    for a in reversed(range(chan // 2)):
        target = column ^ (2 * a)
        beside = swapped(out_block(gating, w_out, target ^ 1, chan), "chan", 1)
        summed = out_block(gating, w_out, target, chan).astype(jnp.float32) + beside.astype(jnp.float32)
        if a:
            summed = swapped(summed.astype(jnp.bfloat16), "chan", 2 * a).astype(jnp.float32)
        total += summed
    return total.astype(jnp.bfloat16)


def solution(mesh):
    in_specs = (
        P("seq", "chan"),
        P(),
        P("seq", None, "chan"),
        P(None, None, "chan"),
        P(None, "chan"),
        P("chan"),
        P("chan", None),
    )
    out_specs = P("seq", "chan")
    return jax.shard_map(
        per_device, mesh=mesh, in_specs=in_specs, out_specs=out_specs, check_vma=False
    )
```

```python
import jax
import jax.numpy as jnp
from jax import lax
from jax.experimental import pallas as pl
from jax.experimental.pallas import tpu as pltpu
from jax.sharding import PartitionSpec as P

TAPS = 128
GROUP = 16
EDGE = TAPS + 16
PARTS = 2
EPSILON = 1e-06


def swapped(value, axis, bit):
    return lax.ppermute(value, axis, [(i, i ^ bit) for i in range(lax.axis_size(axis))])


def project(order, places, rows, sections, addend, near):
    ranks = len(rows)
    depth = rows[0].shape[1]
    step, width = sections[0].shape
    each = rows[0].shape[0] // near
    span = ranks * each
    count = near * span
    tile = min(count, 256)

    def kernel(order_ref, places_ref, *refs):
        gathered, out_ref = refs[-1], refs[-2]
        for i in range(ranks):
            place = pl.multiple_of(places_ref[i] * each, each)
            for o in range(near):
                gathered[pl.ds(o * span + place, each)] = refs[i][o * each : (o + 1) * each]
        section_refs = refs[ranks : ranks + len(sections)]
        for start in range(0, count, tile):
            here = slice(start, start + tile)
            total = jnp.zeros((tile, width), jnp.float32)
            for i, ref in enumerate(section_refs):
                place = pl.ds(pl.multiple_of(order_ref[i] * step, step), step)
                total += jnp.dot(gathered[here, place], ref[...], preferred_element_type=jnp.float32)
            if addend is not None:
                total += refs[-3][here].astype(jnp.float32)
            out_ref[here] = total.astype(jnp.bfloat16)

    extra = [] if addend is None else [addend]
    smem = pl.BlockSpec(memory_space=pltpu.SMEM)
    vmem = pl.BlockSpec(memory_space=pltpu.VMEM)
    return pl.pallas_call(
        kernel,
        in_specs=[smem, smem] + [vmem] * (ranks + len(sections) + len(extra)),
        out_specs=vmem,
        out_shape=jax.ShapeDtypeStruct((count, width), jnp.bfloat16),
        scratch_shapes=[pltpu.VMEM((count, depth), jnp.bfloat16)],
        compiler_params=pltpu.CompilerParams(vmem_limit_bytes=32 << 20),
        cost_estimate=pl.CostEstimate(
            flops=2 * count * depth * width,
            bytes_accessed=2 * (count * depth + depth * width + count * width),
            transcendentals=0,
        ),
        name="project",
    )(order, places, *rows, *sections, *extra)


def gate(halo, parts, short_taps, skip_gain, toeplitz):
    slots, part_rows, wide = parts[0].shape
    width = wide // 3
    row_count = part_rows * len(parts)
    filters = toeplitz.shape[1] // (2 * TAPS)

    def kernel(halo_ref, *refs):
        part_refs = refs[: len(parts)]
        taps_ref, skip_ref, toeplitz_ref, out_ref, extended = refs[len(parts) :]
        extended[:EDGE] = halo_ref[0].astype(jnp.float32)
        for i, ref in enumerate(part_refs):
            extended[EDGE + i * part_rows : EDGE + (i + 1) * part_rows] = ref[0].astype(jnp.float32)
        rows = TAPS + row_count
        filtered = sum(
            taps_ref[lag : lag + 1] * extended[16 - lag : 16 - lag + rows] for lag in range(3)
        )
        product = filtered[:, width : 2 * width] * filtered[:, 2 * width :]
        product = product.astype(jnp.bfloat16)
        owner = lax.broadcasted_iota(jnp.int32, (2 * TAPS, width), 1) // GROUP
        for start in range(0, row_count, TAPS):
            window = product[start : start + 2 * TAPS]
            spread = jnp.concatenate(
                [jnp.where(owner == f, window, jnp.zeros_like(window)) for f in range(filters)], 0
            )
            convolved = jnp.dot(toeplitz_ref[...], spread, preferred_element_type=jnp.float32)
            mixing = skip_ref[...] * window[TAPS:].astype(jnp.float32) + convolved
            queries = filtered[TAPS + start : 2 * TAPS + start, :width]
            out_ref[0, start : start + TAPS] = (queries * mixing).astype(jnp.bfloat16)

    slot = lambda i: (i, 0, 0)
    fixed = lambda i: (0, 0)
    return pl.pallas_call(
        kernel,
        grid=(slots,),
        in_specs=[pl.BlockSpec((1, EDGE, wide), slot)]
        + [pl.BlockSpec((1, part_rows, wide), slot)] * len(parts)
        + [
            pl.BlockSpec((3, wide), fixed),
            pl.BlockSpec((1, width), fixed),
            pl.BlockSpec((TAPS, 2 * TAPS * filters), fixed),
        ],
        out_specs=pl.BlockSpec((1, row_count, width), slot),
        out_shape=jax.ShapeDtypeStruct((slots, row_count, width), jnp.bfloat16),
        scratch_shapes=[pltpu.VMEM((EDGE + row_count, wide), jnp.float32)],
        compiler_params=pltpu.CompilerParams(vmem_limit_bytes=40 << 20),
        cost_estimate=pl.CostEstimate(
            flops=2 * slots * row_count * 2 * TAPS * filters * width,
            bytes_accessed=2 * slots * row_count * 4 * width,
            transcendentals=0,
        ),
        name="gate",
    )(halo, *parts, short_taps, skip_gain, toeplitz)


def out_block(gating, w_out, block, count):
    rows, depth = gating.shape
    columns = w_out.shape[1] // count
    tile = min(columns, 512)
    steps = columns // tile

    def kernel(block_ref, gating_ref, w_ref, out_ref):
        out_ref[...] = jnp.dot(
            gating_ref[...], w_ref[...], preferred_element_type=jnp.float32
        ).astype(jnp.bfloat16)

    return pl.pallas_call(
        kernel,
        grid_spec=pltpu.PrefetchScalarGridSpec(
            num_scalar_prefetch=1,
            grid=(steps,),
            in_specs=[
                pl.BlockSpec((rows, depth), lambda i, b: (0, 0)),
                pl.BlockSpec((depth, tile), lambda i, b: (0, b[0] * steps + i)),
            ],
            out_specs=pl.BlockSpec((rows, tile), lambda i, b: (0, i)),
        ),
        out_shape=jax.ShapeDtypeStruct((rows, columns), jnp.bfloat16),
        compiler_params=pltpu.CompilerParams(vmem_limit_bytes=40 << 20),
        cost_estimate=pl.CostEstimate(
            flops=2 * rows * depth * columns,
            bytes_accessed=2 * (rows * depth + depth * columns + rows * columns),
            transcendentals=0,
        ),
        name="out_block",
    )(block.reshape(1).astype(jnp.int32), gating, w_out)


def toeplitz_of(medium_taps):
    cube_shape = (TAPS, TAPS, 2 * TAPS)
    lagged = (
        lax.broadcasted_iota(jnp.int32, cube_shape, 1)
        + TAPS
        - lax.broadcasted_iota(jnp.int32, cube_shape, 2)
    )
    onehot = (lagged == lax.broadcasted_iota(jnp.int32, cube_shape, 0)).astype(jnp.bfloat16)
    return jnp.einsum("jg,jis->igs", medium_taps.astype(jnp.bfloat16), onehot)


def per_device(tokens, norm_gain, w_in, short_taps, medium_taps, skip_gain, w_out):
    seq, chan = lax.axis_size("seq"), lax.axis_size("chan")
    here, column = lax.axis_index("seq"), lax.axis_index("chan")
    near = seq // 4
    odd, layer = here % 2, here // 2
    half, place = layer // near, layer % near
    row_count = tokens.shape[0]
    depth = norm_gain.shape[0]
    channels = w_in.shape[2]
    mine = channels // near
    pieces = max(1, mine // 128)
    width = mine // pieces
    part_rows = row_count // PARTS

    ranks = chan
    each = part_rows // ranks
    order = jnp.stack([(place ^ o) * 2 + (odd ^ p) for o in range(near) for p in range(2)])
    order = order.astype(jnp.int32)
    places = jnp.stack([column ^ i for i in range(ranks)]).astype(jnp.int32)

    def cut(i, o):
        start = (place ^ o) * mine + i * width
        return lax.dynamic_slice_in_dim(w_in, start, width, 2).reshape(w_in.shape[0], 3 * width)

    def share_out(part):
        parts = [lax.dynamic_slice_in_dim(part, (column ^ i) * each, each, 0) for i in range(ranks)]
        return [rows if i == 0 else swapped(rows, "chan", i) for i, rows in enumerate(parts)]

    def normed_halves(pieces):
        widened = [piece.astype(jnp.float32) for piece in pieces]
        square = sum(jnp.sum(piece * piece, axis=1, keepdims=True) for piece in widened)
        scale = lax.rsqrt(square / depth + EPSILON)
        gains = norm_gain.reshape(ranks, 1, depth // ranks)
        normed = jnp.stack(
            [
                (piece * scale * lax.dynamic_index_in_dim(gains, column ^ i, 0, False)).astype(jnp.bfloat16)
                for i, piece in enumerate(widened)
            ]
        )

        def of_half(which):
            chosen = [
                lax.dynamic_index_in_dim(normed, column ^ (which * (ranks // 2) + i), 0, False)
                for i in range(ranks // 2)
            ]
            return jnp.concatenate(chosen, 1)

        return of_half(half), of_half(1 - half)

    def near_rows(rows):
        return jnp.concatenate(
            [rows if o == 0 else swapped(rows, "seq", 2 * o) for o in range(near)], 0
        )

    def chan_rows(rows):
        across = [rows if a == 0 else swapped(rows, "chan", 2 * a) for a in range(ranks // 2)]
        return [moved for value in across for moved in (value, swapped(value, "chan", 1))]

    def near_cuts(cuts):
        return [value if o == 0 else swapped(value, "seq", 2 * o) for o, value in enumerate(cuts)]

    hold = lax.optimization_barrier
    cuts = [[cut(i, o) for o in range(near)] for i in range(pieces)]
    parts = [tokens[i * part_rows : (i + 1) * part_rows] for i in range(PARTS)]

    def paired(i):
        return swapped(cuts[i][0], "seq", 1)

    def paired_near(i):
        return [swapped(value, "seq", 1) for value in nears[i][1:]]

    nears, own_pair, near_pair = [None] * pieces, [None] * pieces, [None] * pieces
    away, kept = [None] * PARTS, [None] * PARTS
    away_rows, own_rows = [None] * PARTS, [None] * PARTS
    sums = [[None] * PARTS for _ in range(pieces)]
    moved = [[None] * PARTS for _ in range(pieces)]

    def sections(i):
        both = []
        for o in range(near):
            both += [nears[i][o], own_pair[i] if o == 0 else near_pair[i][o - 1]]
        return both

    def send_partial(i, j):
        sent = project(order, places, away_rows[j], sections(i), None, near)
        moved[i][j] = swapped(sent, "seq", 2 * near)

    def add_partial(i, j):
        sums[i][j] = project(order, places, own_rows[j], sections(i), moved[i][j], near)

    last = pieces - 1
    two = min(1, last)
    shared = share_out(parts[0])
    own_pair[0] = paired(0)
    nears[0] = near_cuts(cuts[0])
    shared, own_pair, nears, cuts, parts = hold((shared, own_pair, nears, cuts, parts))
    kept[0], send = normed_halves(shared)
    away[0] = swapped(send, "seq", 2 * near)
    shared = share_out(parts[1])
    near_pair[0] = paired_near(0)
    kept, away, shared, near_pair, cuts = hold((kept, away, shared, near_pair, cuts))
    kept[1], send = normed_halves(shared)
    away[1] = swapped(send, "seq", 2 * near)
    away[0] = near_rows(away[0])
    if last > 0:
        own_pair[1] = paired(1)
        nears[1] = near_cuts(cuts[1])
    kept, away, own_pair, nears, cuts = hold((kept, away, own_pair, nears, cuts))
    away_rows[0] = chan_rows(away[0])
    away[1] = near_rows(away[1])
    if last > 0:
        near_pair[1] = paired_near(1)
    if last > 1:
        nears[2] = near_cuts(cuts[2])
    kept, away, away_rows, near_pair, nears, cuts = hold(
        (kept, away, away_rows, near_pair, nears, cuts)
    )
    send_partial(0, 0)
    away_rows[1] = chan_rows(away[1])
    kept[0] = near_rows(kept[0])
    if last > 1:
        own_pair[2] = paired(2)
    if last > 2:
        nears[3] = near_cuts(cuts[3])
    moved, away_rows, kept, own_pair, nears, cuts = hold(
        (moved, away_rows, kept, own_pair, nears, cuts)
    )
    send_partial(0, 1)
    own_rows[0] = chan_rows(kept[0])
    kept[1] = near_rows(kept[1])
    if last > 0:
        send_partial(1, 0)
    if last > 1:
        near_pair[2] = paired_near(2)
    moved, own_rows, kept, near_pair, cuts = hold((moved, own_rows, kept, near_pair, cuts))
    own_rows[1] = chan_rows(kept[1])
    if last > 0:
        send_partial(1, 1)
    if last > 1:
        send_partial(2, 0)
    if last > 2:
        own_pair[3] = paired(3)
    moved, own_rows, own_pair, nears = hold((moved, own_rows, own_pair, nears))
    if last > 1:
        send_partial(2, 1)
    if last > 2:
        near_pair[3] = paired_near(3)
    moved, near_pair = hold((moved, near_pair))
    if last > 2:
        send_partial(3, 0)
        send_partial(3, 1)
    for i in range(pieces):
        for j in range(PARTS):
            add_partial(i, j)

    short = lax.dynamic_slice_in_dim(short_taps, place * mine, mine, 2)
    skip = lax.dynamic_slice_in_dim(skip_gain, place * mine, mine, 0).reshape(1, mine)
    filters = medium_taps.shape[1] // near
    toeplitz = toeplitz_of(lax.dynamic_slice_in_dim(medium_taps, place * filters, filters, 1))
    some = filters // pieces
    far = [(2 * i + 1, 2 * (near + i)) for i in range(near)]
    gates = []
    for i in range(pieces):
        joined = [value.reshape(near, part_rows, 3 * width) for value in sums[i]]
        edge = joined[-1][:, part_rows - EDGE :]
        edge = jnp.stack([lax.dynamic_index_in_dim(edge, place ^ o, 0, False) for o in range(near)])
        across = swapped(edge, "seq", 1)
        before = jnp.concatenate([lax.ppermute(edge[-1:], "seq", far), across[:-1]], 0)
        halo = jnp.where(odd == 1, across, before)
        halo = jnp.stack([lax.dynamic_index_in_dim(halo, place ^ o, 0, False) for o in range(near)])
        span = slice(i * width, (i + 1) * width)
        gated = gate(
            halo,
            joined,
            short[:, :, span].reshape(3, 3 * width),
            skip[:, span],
            toeplitz[:, i * some : (i + 1) * some].reshape(TAPS, some * 2 * TAPS),
        )
        gates.append([gated[0]] + [swapped(gated[o], "seq", 2 * o) for o in range(1, near)])
    gating = jnp.zeros((row_count, channels), jnp.bfloat16)
    for o in range(near):
        share = jnp.concatenate([piece[o] for piece in gates], 1)
        gating = lax.dynamic_update_slice(gating, share, (0, (place ^ o) * mine))

    total = tokens.astype(jnp.float32)
    for a in reversed(range(chan // 2)):
        target = column ^ (2 * a)
        beside = swapped(out_block(gating, w_out, target ^ 1, chan), "chan", 1)
        summed = out_block(gating, w_out, target, chan).astype(jnp.float32) + beside.astype(jnp.float32)
        if a:
            summed = swapped(summed.astype(jnp.bfloat16), "chan", 2 * a).astype(jnp.float32)
        total += summed
    return total.astype(jnp.bfloat16)


def solution(mesh):
    in_specs = (
        P("seq", "chan"),
        P(),
        P("seq", None, "chan"),
        P(None, None, "chan"),
        P(None, "chan"),
        P("chan"),
        P("chan", None),
    )
    out_specs = P("seq", "chan")
    return jax.shard_map(
        per_device, mesh=mesh, in_specs=in_specs, out_specs=out_specs, check_vma=False
    )
```

```python
import jax
import jax.numpy as jnp
from jax import lax
from jax.experimental import pallas as pl
from jax.experimental.pallas import tpu as pltpu
from jax.sharding import PartitionSpec as P

TAPS = 128
GROUP = 16
EDGE = TAPS + 16
EPSILON = 1e-06


def swapped(value, axis, bit):
    return lax.ppermute(value, axis, [(i, i ^ bit) for i in range(lax.axis_size(axis))])


def project(order, places, rows, sections, addend, near):
    ranks = len(rows)
    depth = rows[0].shape[1]
    step, width = sections[0].shape
    each = rows[0].shape[0] // near
    span = ranks * each
    count = near * span
    tile = count if count <= 256 else count // 2

    def kernel(order_ref, places_ref, *refs):
        gathered, out_ref = refs[-1], refs[-2]
        for i in range(ranks):
            place = pl.multiple_of(places_ref[i] * each, each)
            for o in range(near):
                gathered[pl.ds(o * span + place, each)] = refs[i][o * each : (o + 1) * each]
        section_refs = refs[ranks : ranks + len(sections)]
        for start in range(0, count, tile):
            here = slice(start, start + tile)
            total = jnp.zeros((tile, width), jnp.float32)
            for i, ref in enumerate(section_refs):
                place = pl.ds(pl.multiple_of(order_ref[i] * step, step), step)
                total += jnp.dot(gathered[here, place], ref[...], preferred_element_type=jnp.float32)
            if addend is not None:
                total += refs[-3][here].astype(jnp.float32)
            out_ref[here] = total.astype(jnp.bfloat16)

    extra = [] if addend is None else [addend]
    smem = pl.BlockSpec(memory_space=pltpu.SMEM)
    vmem = pl.BlockSpec(memory_space=pltpu.VMEM)
    return pl.pallas_call(
        kernel,
        in_specs=[smem, smem] + [vmem] * (ranks + len(sections) + len(extra)),
        out_specs=vmem,
        out_shape=jax.ShapeDtypeStruct((count, width), jnp.bfloat16),
        scratch_shapes=[pltpu.VMEM((count, depth), jnp.bfloat16)],
        compiler_params=pltpu.CompilerParams(vmem_limit_bytes=32 << 20),
        cost_estimate=pl.CostEstimate(
            flops=2 * count * depth * width,
            bytes_accessed=2 * (count * depth + depth * width + count * width),
            transcendentals=0,
        ),
        name="project",
    )(order, places, *rows, *sections, *extra)


def gate(inputs, spans, row_count, short_taps, skip_gain, toeplitz):
    slots, _, wide = inputs[0].shape
    width = wide // 3
    filters = toeplitz.shape[1] // (2 * TAPS)
    reach = max(row_count, TAPS)

    def kernel(*refs):
        input_refs = refs[: len(inputs)]
        taps_ref, skip_ref, toeplitz_ref, out_ref, extended = refs[len(inputs) :]
        end = 0
        for ref, (first, last) in zip(input_refs, spans, strict=True):
            extended[end : end + last - first] = ref[0, first:last].astype(jnp.float32)
            end += last - first
        if row_count < TAPS:
            extended[end:] = jnp.zeros((TAPS - row_count, wide), jnp.float32)
        rows = TAPS + reach
        filtered = sum(
            taps_ref[lag : lag + 1] * extended[16 - lag : 16 - lag + rows] for lag in range(3)
        )
        product = filtered[:, width : 2 * width] * filtered[:, 2 * width :]
        product = product.astype(jnp.bfloat16)
        owner = lax.broadcasted_iota(jnp.int32, (2 * TAPS, width), 1) // GROUP
        for start in range(0, row_count, TAPS):
            start = min(start, reach - TAPS)
            size = min(TAPS, row_count)
            window = product[start : start + 2 * TAPS]
            spread = jnp.concatenate(
                [jnp.where(owner == f, window, jnp.zeros_like(window)) for f in range(filters)], 0
            )
            convolved = jnp.dot(toeplitz_ref[...], spread, preferred_element_type=jnp.float32)
            mixing = skip_ref[...] * window[TAPS:].astype(jnp.float32) + convolved
            queries = filtered[TAPS + start : 2 * TAPS + start, :width]
            out_ref[0, start : start + size] = (queries * mixing)[:size].astype(jnp.bfloat16)

    slot = lambda i: (i, 0, 0)
    fixed = lambda i: (0, 0)
    return pl.pallas_call(
        kernel,
        grid=(slots,),
        in_specs=[pl.BlockSpec((1,) + value.shape[1:], slot) for value in inputs]
        + [
            pl.BlockSpec((3, wide), fixed),
            pl.BlockSpec((1, width), fixed),
            pl.BlockSpec((TAPS, 2 * TAPS * filters), fixed),
        ],
        out_specs=pl.BlockSpec((1, row_count, width), slot),
        out_shape=jax.ShapeDtypeStruct((slots, row_count, width), jnp.bfloat16),
        scratch_shapes=[pltpu.VMEM((EDGE + reach, wide), jnp.float32)],
        compiler_params=pltpu.CompilerParams(vmem_limit_bytes=40 << 20),
        cost_estimate=pl.CostEstimate(
            flops=2 * slots * row_count * 2 * TAPS * filters * width,
            bytes_accessed=2 * slots * row_count * 4 * width,
            transcendentals=0,
        ),
        name="gate",
    )(*inputs, short_taps, skip_gain, toeplitz)


def out_block(gating, w_out, block, count):
    rows, depth = gating.shape
    columns = w_out.shape[1] // count
    tile = min(columns, 512)
    steps = columns // tile

    def kernel(block_ref, gating_ref, w_ref, out_ref):
        out_ref[...] = jnp.dot(
            gating_ref[...], w_ref[...], preferred_element_type=jnp.float32
        ).astype(jnp.bfloat16)

    return pl.pallas_call(
        kernel,
        grid_spec=pltpu.PrefetchScalarGridSpec(
            num_scalar_prefetch=1,
            grid=(steps,),
            in_specs=[
                pl.BlockSpec((rows, depth), lambda i, b: (0, 0)),
                pl.BlockSpec((depth, tile), lambda i, b: (0, b[0] * steps + i)),
            ],
            out_specs=pl.BlockSpec((rows, tile), lambda i, b: (0, i)),
        ),
        out_shape=jax.ShapeDtypeStruct((rows, columns), jnp.bfloat16),
        compiler_params=pltpu.CompilerParams(vmem_limit_bytes=40 << 20),
        cost_estimate=pl.CostEstimate(
            flops=2 * rows * depth * columns,
            bytes_accessed=2 * (rows * depth + depth * columns + rows * columns),
            transcendentals=0,
        ),
        name="out_block",
    )(block.reshape(1).astype(jnp.int32), gating, w_out)


def toeplitz_of(medium_taps):
    cube_shape = (TAPS, TAPS, 2 * TAPS)
    lagged = (
        lax.broadcasted_iota(jnp.int32, cube_shape, 1)
        + TAPS
        - lax.broadcasted_iota(jnp.int32, cube_shape, 2)
    )
    onehot = (lagged == lax.broadcasted_iota(jnp.int32, cube_shape, 0)).astype(jnp.bfloat16)
    return jnp.einsum("jg,jis->igs", medium_taps.astype(jnp.bfloat16), onehot)


def row_parts(row_count, ranks):
    unit = 16 * ranks
    units = row_count // unit
    low = max(1, units // 4)
    middle = (units - low) // 2
    sizes = [size * unit for size in (units - low - middle, middle, low) if size]
    ends = [row_count - sum(sizes[:i]) for i in range(len(sizes))]
    return [(end - size, end) for end, size in zip(ends, sizes, strict=True)]


def per_device(tokens, norm_gain, w_in, short_taps, medium_taps, skip_gain, w_out):
    seq, ranks = lax.axis_size("seq"), lax.axis_size("chan")
    here, column = lax.axis_index("seq"), lax.axis_index("chan")
    near = seq // 4
    odd, layer = here % 2, here // 2
    half, place = layer // near, layer % near
    row_count = tokens.shape[0]
    depth = norm_gain.shape[0]
    channels = w_in.shape[2]
    mine = channels // near
    pieces = max(1, mine // 256)
    width = mine // pieces
    parts = row_parts(row_count, ranks)
    slab = w_in.shape[0] // 2
    order = jnp.stack(
        [((place ^ o) * 2 + (odd ^ p)) * 2 + h for o in range(near) for p in range(2) for h in range(2)]
    ).astype(jnp.int32)
    places = jnp.stack([column ^ i for i in range(ranks)]).astype(jnp.int32)
    state = {"tokens": tokens, "w_in": w_in}
    fresh = {}

    def cut(i, o, h):
        rows = state["w_in"][h * slab : (h + 1) * slab]
        start = (place ^ o) * mine + i * width
        return lax.dynamic_slice_in_dim(rows, start, width, 2).reshape(slab, 3 * width)

    def near_w(i, h):
        if i < pieces:
            for o in range(1, near):
                state["w", i, o, 0, h] = swapped(cut(i, o, h), "seq", 2 * o)

    def pair_own_w(i, h):
        if i < pieces:
            state["w", i, 0, 0, h] = own = cut(i, 0, h)
            state["w", i, 0, 1, h] = swapped(own, "seq", 1)

    def pair_near_w(i, h):
        if i < pieces:
            for o in range(1, near):
                state["w", i, o, 1, h] = swapped(state["w", i, o, 0, h], "seq", 1)

    def share(j):
        if j < len(parts):
            first, last = parts[j]
            part = state["tokens"][first:last]
            each = (last - first) // ranks
            for r in range(ranks):
                rows = lax.dynamic_slice_in_dim(part, (column ^ r) * each, each, 0)
                state["shared", j, r] = rows if r == 0 else swapped(rows, "chan", r)

    def norm_and_cross(j):
        if j >= len(parts):
            return
        widened = [state.pop(("shared", j, r)).astype(jnp.float32) for r in range(ranks)]
        square = sum(jnp.sum(piece * piece, axis=1, keepdims=True) for piece in widened)
        scale = lax.rsqrt(square / depth + EPSILON)
        gains = norm_gain.reshape(ranks, 1, depth // ranks)
        normed = jnp.stack(
            [
                (piece * scale * lax.dynamic_index_in_dim(gains, column ^ r, 0, False)).astype(jnp.bfloat16)
                for r, piece in enumerate(widened)
            ]
        )

        def of_half(which):
            chosen = [
                lax.dynamic_index_in_dim(normed, column ^ (which * (ranks // 2) + r), 0, False)
                for r in range(ranks // 2)
            ]
            return jnp.concatenate(chosen, 1)

        state["kept", j] = of_half(half)
        state["away", j] = swapped(of_half(1 - half), "seq", 2 * near)

    def near_rows(kind, j):
        if j < len(parts):
            rows = state[kind, j]
            moved = [rows if o == 0 else swapped(rows, "seq", 2 * o) for o in range(near)]
            state[kind, j] = jnp.concatenate(moved, 0)

    def across(kind, j):
        if j < len(parts):
            rows = state.pop((kind, j))
            for a in range(ranks // 2):
                state["row", kind, j, 2 * a] = rows if a == 0 else swapped(rows, "chan", 2 * a)
            state["row", kind, j, 1] = swapped(rows, "chan", 1)

    def beside(kind, j):
        if j < len(parts):
            for a in range(1, ranks // 2):
                state["row", kind, j, 2 * a + 1] = swapped(state["row", kind, j, 2 * a], "chan", 1)

    def multiplied(kind, i, j, addend):
        rows = [state["row", kind, j, r] for r in range(ranks)]
        sections = [state["w", i, o, p, h] for o in range(near) for p in range(2) for h in range(2)]
        return project(order, places, rows, sections, addend, near)

    def partial(i, j):
        if i < pieces and j < len(parts):
            state["partial", i, j] = multiplied("away", i, j, None)

    def send(i, j):
        if i < pieces and j < len(parts):
            fresh["moved", i, j] = swapped(state.pop(("partial", i, j)), "seq", 2 * near)

    def add(i, j):
        if i < pieces and j < len(parts):
            total = multiplied("kept", i, j, state.pop(("moved", i, j)))
            state["sum", i, j] = total.reshape(near, parts[j][1] - parts[j][0], 3 * width)

    def step():
        held = lax.optimization_barrier(list(state.values()))
        state.update(zip(list(state), held, strict=True))
        state.update(fresh)
        fresh.clear()

    share(0)
    pair_own_w(0, 0)
    near_w(0, 0)
    step()
    norm_and_cross(0)
    share(1)
    pair_own_w(0, 1)
    near_w(0, 1)
    step()
    norm_and_cross(1)
    near_rows("away", 0)
    share(2)
    pair_near_w(0, 0)
    step()
    norm_and_cross(2)
    across("away", 0)
    near_rows("away", 1)
    pair_near_w(0, 1)
    step()
    beside("away", 0)
    partial(0, 0)
    across("away", 1)
    near_rows("away", 2)
    near_rows("kept", 0)
    near_w(1, 0)
    pair_own_w(1, 0)
    step()
    send(0, 0)
    beside("away", 1)
    partial(0, 1)
    across("away", 2)
    near_rows("kept", 1)
    near_w(1, 1)
    pair_own_w(1, 1)
    step()
    send(0, 1)
    beside("away", 2)
    partial(0, 2)
    across("kept", 0)
    near_rows("kept", 2)
    pair_near_w(1, 0)
    step()
    send(0, 2)
    beside("kept", 0)
    across("kept", 1)
    pair_near_w(1, 1)
    add(0, 0)
    step()
    partial(1, 0)
    send(1, 0)
    beside("kept", 1)
    across("kept", 2)
    step()
    partial(1, 1)
    send(1, 1)
    beside("kept", 2)
    add(0, 1)
    step()
    partial(1, 2)
    send(1, 2)
    add(1, 0)
    add(0, 2)
    step()
    add(1, 1)

    short = lax.dynamic_slice_in_dim(short_taps, place * mine, mine, 2)
    skip = lax.dynamic_slice_in_dim(skip_gain, place * mine, mine, 0).reshape(1, mine)
    filters = medium_taps.shape[1] // near
    toeplitz = toeplitz_of(lax.dynamic_slice_in_dim(medium_taps, place * filters, filters, 1))
    some = filters // pieces
    far = [(2 * i + 1, 2 * (near + i)) for i in range(near)]

    def halo(i):
        edge = state["sum", i, 0][:, -EDGE:]
        edge = jnp.stack([lax.dynamic_index_in_dim(edge, place ^ o, 0, False) for o in range(near)])
        other = swapped(edge, "seq", 1)
        before = jnp.concatenate([lax.ppermute(edge[-1:], "seq", far), other[:-1]], 0)
        rows = jnp.where(odd == 1, other, before)
        return jnp.stack([lax.dynamic_index_in_dim(rows, place ^ o, 0, False) for o in range(near)])

    halos = [halo(i) for i in range(pieces)]
    low = parts[-1][1] + EDGE

    def gated(i, inputs, spans, rows):
        span = slice(i * width, (i + 1) * width)
        return gate(
            inputs,
            spans,
            rows,
            short[:, :, span].reshape(3, 3 * width),
            skip[:, span],
            toeplitz[:, i * some : (i + 1) * some].reshape(TAPS, some * 2 * TAPS),
        )

    def finished(gates, first, last):
        rows = last - first
        gating = jnp.zeros((rows, channels), jnp.bfloat16)
        for o in range(near):
            moved = [piece[o] if o == 0 else swapped(piece[o], "seq", 2 * o) for piece in gates]
            shares = jnp.concatenate(moved, 1)
            gating = lax.dynamic_update_slice(gating, shares, (0, (place ^ o) * mine))
        total = tokens[first:last].astype(jnp.float32)
        for a in reversed(range(ranks // 2)):
            target = column ^ (2 * a)
            added = swapped(out_block(gating, w_out, target ^ 1, ranks), "chan", 1)
            summed = out_block(gating, w_out, target, ranks).astype(jnp.float32) + added.astype(jnp.float32)
            if a:
                summed = swapped(summed.astype(jnp.bfloat16), "chan", 2 * a).astype(jnp.float32)
            total += summed
        return total.astype(jnp.bfloat16)

    gates = []
    for i in range(pieces):
        inputs = [state["sum", i, j] for j in reversed(range(len(parts) - 1))]
        gates.append(gated(i, inputs, [(0, value.shape[1]) for value in inputs], row_count - low))
    upper = finished(gates, low, row_count)
    add(1, 2)
    gates = []
    for i in range(pieces):
        lowest, next_up = state["sum", i, len(parts) - 1], state["sum", i, len(parts) - 2]
        spans = [(0, EDGE), (0, lowest.shape[1]), (0, EDGE)]
        gates.append(gated(i, [halos[i], lowest, next_up], spans, low))
    return jnp.concatenate([finished(gates, 0, low), upper], 0)


def solution(mesh):
    in_specs = (
        P("seq", "chan"),
        P(),
        P("seq", None, "chan"),
        P(None, None, "chan"),
        P(None, "chan"),
        P("chan"),
        P("chan", None),
    )
    out_specs = P("seq", "chan")
    return jax.shard_map(
        per_device, mesh=mesh, in_specs=in_specs, out_specs=out_specs, check_vma=False
    )
```

```python
import jax
import jax.numpy as jnp
from jax import lax
from jax.experimental import pallas as pl
from jax.experimental.pallas import tpu as pltpu
from jax.sharding import PartitionSpec as P

TAPS = 128
GROUP = 16
EDGE = TAPS + 16
EPSILON = 1e-06
VMEM = 24 << 20
SHORT = pl.CostEstimate(flops=1, bytes_accessed=1, transcendentals=0)


def swapped(value, axis, bit):
    return lax.ppermute(value, axis, [(i, i ^ bit) for i in range(lax.axis_size(axis))])


def project(order, places, rows, sections, addend, near, ranks):
    depth = rows[0].shape[1]
    slabs = len(sections[0])
    branches, slab, width = sections[0][0].shape
    step = slabs * slab
    each = 2 * rows[0].shape[0] // (ranks * near)
    span = ranks * each
    count = near * span
    wide = branches * width
    flat = [value for section in sections for value in section]

    def kernel(order_ref, places_ref, *refs):
        gathered, total = refs[-2:]
        out_ref = refs[-3]
        for i in range(ranks):
            place = pl.multiple_of(places_ref[i] * each, each)
            for o in range(near):
                start = ((i // 2) * near + o) * each
                gathered[pl.ds(o * span + place, each)] = refs[i % 2][start : start + each]
        for i in range(len(flat)):
            place = pl.multiple_of(order_ref[i // slabs] * step + (i % slabs) * slab, slab)
            part = gathered[:, pl.ds(place, slab)]
            for b in range(branches):
                columns = slice(b * width, (b + 1) * width)
                value = jnp.dot(part, refs[2 + i][b], preferred_element_type=jnp.float32)
                if i == 0 and addend is not None:
                    value += refs[2 + len(flat)][:, columns].astype(jnp.float32)
                if i:
                    value += total[:, columns]
                if i < len(flat) - 1:
                    total[:, columns] = value
                else:
                    out_ref[:, columns] = value.astype(jnp.bfloat16)

    extra = [] if addend is None else [addend]
    smem = pl.BlockSpec(memory_space=pltpu.SMEM)
    vmem = pl.BlockSpec(memory_space=pltpu.VMEM)
    return pl.pallas_call(
        kernel,
        in_specs=[smem, smem] + [vmem] * (2 + len(flat) + len(extra)),
        out_specs=vmem,
        out_shape=jax.ShapeDtypeStruct((count, wide), jnp.bfloat16),
        scratch_shapes=[
            pltpu.VMEM((count, depth), jnp.bfloat16),
            pltpu.VMEM((count, wide), jnp.float32),
        ],
        compiler_params=pltpu.CompilerParams(vmem_limit_bytes=VMEM),
        cost_estimate=SHORT,
        name="project",
    )(order, places, *rows, *flat, *extra)


def gate(inputs, spans, row_count, short_taps, skip_gain, toeplitz):
    slots, _, wide = inputs[0].shape
    width = wide // 3
    filters = toeplitz.shape[1] // (2 * TAPS)
    reach = max(row_count, TAPS)

    def kernel(*refs):
        input_refs = refs[: len(inputs)]
        taps_ref, skip_ref, toeplitz_ref, out_ref, extended = refs[len(inputs) :]
        end = 0
        for ref, (first, last) in zip(input_refs, spans, strict=True):
            extended[end : end + last - first] = ref[0, first:last].astype(jnp.float32)
            end += last - first
        if row_count < TAPS:
            extended[end:] = jnp.zeros((TAPS - row_count, wide), jnp.float32)
        rows = TAPS + reach
        filtered = sum(
            taps_ref[lag : lag + 1] * extended[16 - lag : 16 - lag + rows] for lag in range(3)
        )
        product = filtered[:, width : 2 * width] * filtered[:, 2 * width :]
        product = product.astype(jnp.bfloat16)
        owner = lax.broadcasted_iota(jnp.int32, (2 * TAPS, width), 1) // GROUP
        for start in range(0, row_count, TAPS):
            start = min(start, reach - TAPS)
            size = min(TAPS, row_count)
            window = product[start : start + 2 * TAPS]
            spread = jnp.concatenate(
                [jnp.where(owner == f, window, jnp.zeros_like(window)) for f in range(filters)], 0
            )
            convolved = jnp.dot(toeplitz_ref[...], spread, preferred_element_type=jnp.float32)
            mixing = skip_ref[...] * window[TAPS:].astype(jnp.float32) + convolved
            queries = filtered[TAPS + start : 2 * TAPS + start, :width]
            out_ref[0, start : start + size] = (queries * mixing)[:size].astype(jnp.bfloat16)

    slot = lambda i: (i, 0, 0)
    fixed = lambda i: (0, 0)
    return pl.pallas_call(
        kernel,
        grid=(slots,),
        in_specs=[pl.BlockSpec((1,) + value.shape[1:], slot) for value in inputs]
        + [
            pl.BlockSpec((3, wide), fixed),
            pl.BlockSpec((1, width), fixed),
            pl.BlockSpec((TAPS, 2 * TAPS * filters), fixed),
        ],
        out_specs=pl.BlockSpec((1, row_count, width), slot),
        out_shape=jax.ShapeDtypeStruct((slots, row_count, width), jnp.bfloat16),
        scratch_shapes=[pltpu.VMEM((EDGE + reach, wide), jnp.float32)],
        compiler_params=pltpu.CompilerParams(vmem_limit_bytes=VMEM),
        cost_estimate=SHORT,
        name="gate",
    )(*inputs, short_taps, skip_gain, toeplitz)


def out_block(gating, w_out, block, count):
    rows, depth = gating.shape
    columns = w_out.shape[1] // count
    tile = min(columns, 512)
    steps = columns // tile

    def kernel(block_ref, gating_ref, w_ref, out_ref):
        out_ref[...] = jnp.dot(
            gating_ref[...], w_ref[...], preferred_element_type=jnp.float32
        ).astype(jnp.bfloat16)

    return pl.pallas_call(
        kernel,
        grid_spec=pltpu.PrefetchScalarGridSpec(
            num_scalar_prefetch=1,
            grid=(steps,),
            in_specs=[
                pl.BlockSpec((rows, depth), lambda i, b: (0, 0)),
                pl.BlockSpec((depth, tile), lambda i, b: (0, b[0] * steps + i)),
            ],
            out_specs=pl.BlockSpec((rows, tile), lambda i, b: (0, i)),
        ),
        out_shape=jax.ShapeDtypeStruct((rows, columns), jnp.bfloat16),
        compiler_params=pltpu.CompilerParams(vmem_limit_bytes=VMEM),
        cost_estimate=SHORT,
        name="out_block",
    )(block.reshape(1).astype(jnp.int32), gating, w_out)


def toeplitz_of(medium_taps):
    cube_shape = (TAPS, TAPS, 2 * TAPS)
    lagged = (
        lax.broadcasted_iota(jnp.int32, cube_shape, 1)
        + TAPS
        - lax.broadcasted_iota(jnp.int32, cube_shape, 2)
    )
    onehot = (lagged == lax.broadcasted_iota(jnp.int32, cube_shape, 0)).astype(jnp.bfloat16)
    return jnp.einsum("jg,jis->igs", medium_taps.astype(jnp.bfloat16), onehot)


def row_parts(row_count, ranks):
    unit = 16 * ranks
    units = row_count // unit
    low = max(1, units // 4)
    middle = (units - low) // 2
    sizes = [size * unit for size in (units - low - middle, middle, low) if size]
    ends = [row_count - sum(sizes[:i]) for i in range(len(sizes))]
    return [(end - size, end) for end, size in zip(ends, sizes, strict=True)]


def per_device(tokens, norm_gain, w_in, short_taps, medium_taps, skip_gain, w_out):
    seq, ranks = lax.axis_size("seq"), lax.axis_size("chan")
    here, column = lax.axis_index("seq"), lax.axis_index("chan")
    near = seq // 4
    odd, layer = here % 2, here // 2
    half, place = layer // near, layer % near
    row_count = tokens.shape[0]
    depth = norm_gain.shape[0]
    channels = w_in.shape[2]
    mine = channels // near
    pieces = max(1, mine // 256)
    width = mine // pieces
    parts = row_parts(row_count, ranks)
    slab = w_in.shape[0] // 2
    order = jnp.stack(
        [(place ^ o) * 2 + (odd ^ p) for o in range(near) for p in range(2)]
    ).astype(jnp.int32)
    places = jnp.stack([column ^ i for i in range(ranks)]).astype(jnp.int32)
    state = {}

    def cut(i, o, h):
        if h not in state:
            rows = jnp.transpose(w_in[h * slab : (h + 1) * slab], (1, 0, 2))
            state[h] = lax.optimization_barrier(rows)
        return lax.dynamic_slice_in_dim(state[h], (place ^ o) * mine + i * width, width, 2)

    def near_w(i, h):
        if i < pieces:
            for o in range(1, near):
                state["w", i, o, 0, h] = swapped(cut(i, o, h), "seq", 2 * o)

    def pair_own_w(i, h):
        if i < pieces:
            state["w", i, 0, 0, h] = own = cut(i, 0, h)
            state["w", i, 0, 1, h] = swapped(own, "seq", 1)

    def pair_near_w(i, h):
        if i < pieces:
            for o in range(1, near):
                state["w", i, o, 1, h] = swapped(state["w", i, o, 0, h], "seq", 1)

    def share():
        cuts = []
        for r in range(ranks):
            rows = []
            for first, last in parts:
                size = (last - first) // ranks
                rows.append(lax.dynamic_slice_in_dim(tokens, first + (column ^ r) * size, size, 0))
            cuts.append(jnp.concatenate(rows, 0))
        for r in range(ranks):
            state["shared", r] = cuts[r] if r == 0 else swapped(cuts[r], "chan", r)

    def norm(j):
        if j >= len(parts):
            return
        start = (row_count - parts[j][1]) // ranks
        size = (parts[j][1] - parts[j][0]) // ranks
        widened = [state["shared", r][start : start + size].astype(jnp.float32) for r in range(ranks)]
        square = sum(jnp.sum(piece * piece, axis=1, keepdims=True) for piece in widened)
        scale = lax.rsqrt(square / depth + EPSILON)
        gains = norm_gain.reshape(ranks, 1, depth // ranks)
        normed = jnp.stack(
            [
                (piece * scale * lax.dynamic_index_in_dim(gains, column ^ r, 0, False)).astype(jnp.bfloat16)
                for r, piece in enumerate(widened)
            ]
        )

        def of_half(which):
            chosen = [
                lax.dynamic_index_in_dim(normed, column ^ (which * (ranks // 2) + r), 0, False)
                for r in range(ranks // 2)
            ]
            return jnp.concatenate(chosen, 1)

        state["kept", j] = of_half(half)
        state["away", j] = of_half(1 - half)

    def cross(j):
        if j < len(parts):
            state["away", j] = swapped(state["away", j], "seq", 2 * near)

    def near_rows(kind, j):
        if j < len(parts):
            rows = state[kind, j]
            moved = [rows if o == 0 else swapped(rows, "seq", 2 * o) for o in range(near)]
            state[kind, j] = jnp.concatenate(moved, 0)

    def across(kind, j):
        if j < len(parts):
            rows = state[kind, j]
            moved = [rows if a == 0 else swapped(rows, "chan", 2 * a) for a in range(ranks // 2)]
            state[kind, j] = jnp.concatenate(moved, 0)

    def beside(kind, j):
        if j < len(parts):
            state["other", kind, j] = swapped(state[kind, j], "chan", 1)

    def multiplied(kind, i, j, addend):
        rows = [state[kind, j], state["other", kind, j]]
        sections = [[state["w", i, o, p, h] for h in range(2)] for o in range(near) for p in range(2)]
        return project(order, places, rows, sections, addend, near, ranks)

    def partial(i, j):
        if i < pieces and j < len(parts):
            state["partial", i, j] = multiplied("away", i, j, None)

    def send(i, j):
        if i < pieces and j < len(parts):
            state["moved", i, j] = swapped(state.pop(("partial", i, j)), "seq", 2 * near)

    def add(i, j):
        if i < pieces and j < len(parts):
            total = multiplied("kept", i, j, state.pop(("moved", i, j)))
            state["sum", i, j] = total.reshape(near, parts[j][1] - parts[j][0], 3 * width)

    def constants():
        short = lax.dynamic_slice_in_dim(short_taps, place * mine, mine, 2)
        skip = lax.dynamic_slice_in_dim(skip_gain, place * mine, mine, 0).reshape(1, mine)
        filters = medium_taps.shape[1] // near
        toeplitz = toeplitz_of(lax.dynamic_slice_in_dim(medium_taps, place * filters, filters, 1))
        some = filters // pieces
        for i in range(pieces):
            span = slice(i * width, (i + 1) * width)
            blocks = toeplitz[:, i * some : (i + 1) * some].reshape(TAPS, some * 2 * TAPS)
            state["constants", i, 0] = short[:, :, span].reshape(3, 3 * width)
            state["constants", i, 1] = skip[:, span]
            state["constants", i, 2] = blocks

    def step():
        held = lax.optimization_barrier(list(state.values()))
        state.update(zip(list(state), held, strict=True))

    share()
    pair_own_w(0, 0)
    near_w(0, 0)
    step()
    for j in range(len(parts)):
        norm(j)
    cross(0)
    pair_own_w(0, 1)
    near_w(0, 1)
    step()
    cross(1)
    constants()
    near_rows("away", 0)
    pair_near_w(0, 0)
    step()
    cross(2)
    across("away", 0)
    near_rows("away", 1)
    pair_near_w(0, 1)
    step()
    beside("away", 0)
    partial(0, 0)
    across("away", 1)
    near_rows("away", 2)
    near_w(1, 0)
    pair_own_w(1, 0)
    step()
    send(0, 0)
    beside("away", 1)
    partial(0, 1)
    across("away", 2)
    near_w(1, 1)
    pair_own_w(1, 1)
    step()
    send(0, 1)
    beside("away", 2)
    partial(0, 2)
    near_rows("kept", 0)
    pair_near_w(1, 0)
    step()
    send(0, 2)
    across("kept", 0)
    near_rows("kept", 1)
    pair_near_w(1, 1)
    step()
    partial(1, 0)
    send(1, 0)
    partial(1, 1)
    beside("kept", 0)
    across("kept", 1)
    near_rows("kept", 2)
    add(0, 0)
    step()
    send(1, 1)
    beside("kept", 1)
    across("kept", 2)
    add(1, 0)
    add(0, 1)
    partial(1, 2)
    step()
    send(1, 2)
    beside("kept", 2)

    far = [(2 * i + 1, 2 * (near + i)) for i in range(near)]

    def halo(i):
        edge = state["sum", i, 0][:, -EDGE:]
        edge = jnp.stack([lax.dynamic_index_in_dim(edge, place ^ o, 0, False) for o in range(near)])
        other = swapped(edge, "seq", 1)
        before = jnp.concatenate([lax.ppermute(edge[-1:], "seq", far), other[:-1]], 0)
        rows = jnp.where(odd == 1, other, before)
        return jnp.stack([lax.dynamic_index_in_dim(rows, place ^ o, 0, False) for o in range(near)])

    low = parts[-1][1] + EDGE

    def gated(i, inputs, spans, rows):
        return gate(inputs, spans, rows, *[state["constants", i, k] for k in range(3)])

    def joined(gates, rows):
        gating = jnp.zeros((rows, channels), jnp.bfloat16)
        for o in range(near):
            moved = [piece[o] if o == 0 else swapped(piece[o], "seq", 2 * o) for piece in gates]
            shares = jnp.concatenate(moved, 1)
            gating = lax.dynamic_update_slice(gating, shares, (0, (place ^ o) * mine))
        return gating

    def chip_sum(gating, a):
        target = column ^ (2 * a)
        other = swapped(out_block(gating, w_out, target ^ 1, ranks), "chan", 1)
        return out_block(gating, w_out, target, ranks).astype(jnp.float32) + other.astype(jnp.float32)

    def far_sums(gating):
        return [chip_sum(gating, a).astype(jnp.bfloat16) for a in range(1, ranks // 2)]

    def sent(sums):
        return [swapped(value, "chan", 2 * a) for a, value in enumerate(sums, 1)]

    def added(first, last, own, received):
        total = tokens[first:last].astype(jnp.float32) + own
        return (total + sum(value.astype(jnp.float32) for value in received)).astype(jnp.bfloat16)

    def all_gated(i):
        inputs = [state["sum", i, j] for j in reversed(range(len(parts) - 1))]
        return gated(i, inputs, [(0, value.shape[1]) for value in inputs], row_count - low)

    last = len(parts) - 1
    add(1, 1)
    upper = joined([all_gated(i) for i in range(pieces)], row_count - low)
    upper, *first_halos = lax.optimization_barrier([upper] + [halo(i) for i in range(pieces)])
    upper_sums = far_sums(upper)
    for i in range(pieces):
        if i:
            state["moved", i, last], upper_sums = lax.optimization_barrier((state["moved", i, last], upper_sums))
    upper_received = sent(upper_sums)
    lower = []
    for i in range(pieces):
        if last > 1 or i:
            add(i, last)
        lowest, next_up = state["sum", i, last], state["sum", i, last - 1]
        spans = [(0, EDGE), (0, lowest.shape[1]), (0, EDGE)]
        lower.append(gated(i, [first_halos[i], lowest, next_up], spans, low))
    lower = joined(lower, low)
    lower_sums = far_sums(lower)
    lower_sums, upper_received, lower = lax.optimization_barrier((lower_sums, upper_received, lower))
    lower_received = sent(lower_sums)
    upper = added(low, row_count, chip_sum(upper, 0), upper_received)
    lower = added(0, low, chip_sum(lower, 0), lower_received)
    return jnp.concatenate([lower, upper], 0)


def solution(mesh):
    in_specs = (
        P("seq", "chan"),
        P(),
        P("seq", None, "chan"),
        P(None, None, "chan"),
        P(None, "chan"),
        P("chan"),
        P("chan", None),
    )
    out_specs = P("seq", "chan")
    return jax.shard_map(
        per_device, mesh=mesh, in_specs=in_specs, out_specs=out_specs, check_vma=False
    )
```

```python
import jax
import jax.numpy as jnp
from jax import lax
from jax.experimental import pallas as pl
from jax.experimental.pallas import tpu as pltpu
from jax.sharding import PartitionSpec as P

TAPS = 128
GROUP = 16
EDGE = TAPS + 16
EPSILON = 1e-06
VMEM = 24 << 20
SHORT = pl.CostEstimate(flops=1, bytes_accessed=1, transcendentals=0)


def swapped(value, axis, bit):
    return lax.ppermute(value, axis, [(i, i ^ bit) for i in range(lax.axis_size(axis))])


def project(order, places, rows, sections, near, ranks):
    depth = rows[0].shape[1]
    slabs = len(sections[0])
    branches, slab, width = sections[0][0].shape
    step = slabs * slab
    each = 2 * rows[0].shape[0] // (ranks * near)
    span = ranks * each
    count = near * span
    wide = branches * width
    flat = [value for section in sections for value in section]

    def kernel(order_ref, places_ref, *refs):
        gathered, total = refs[-2:]
        out_ref = refs[-3]
        for i in range(ranks):
            place = pl.multiple_of(places_ref[i] * each, each)
            for o in range(near):
                start = ((i // 2) * near + o) * each
                gathered[pl.ds(o * span + place, each)] = refs[i % 2][start : start + each]
        for i in range(len(flat)):
            place = pl.multiple_of(order_ref[i // slabs] * step + (i % slabs) * slab, slab)
            part = gathered[:, pl.ds(place, slab)]
            for b in range(branches):
                columns = slice(b * width, (b + 1) * width)
                value = jnp.dot(part, refs[2 + i][b], preferred_element_type=jnp.float32)
                if i:
                    value += total[:, columns]
                if i < len(flat) - 1:
                    total[:, columns] = value
                else:
                    out_ref[:, columns] = value.astype(jnp.bfloat16)

    smem = pl.BlockSpec(memory_space=pltpu.SMEM)
    vmem = pl.BlockSpec(memory_space=pltpu.VMEM)
    return pl.pallas_call(
        kernel,
        in_specs=[smem, smem] + [vmem] * (2 + len(flat)),
        out_specs=vmem,
        out_shape=jax.ShapeDtypeStruct((count, wide), jnp.bfloat16),
        scratch_shapes=[
            pltpu.VMEM((count, depth), jnp.bfloat16),
            pltpu.VMEM((count, wide), jnp.float32),
        ],
        compiler_params=pltpu.CompilerParams(vmem_limit_bytes=VMEM),
        cost_estimate=SHORT,
        name="project",
    )(order, places, *rows, *flat)


def gate(terms, spans, row_count, short_taps, skip_gain, toeplitz):
    inputs = [value for term in terms for value in term]
    slots, _, wide = inputs[0].shape
    width = wide // 3
    filters = toeplitz.shape[1] // (2 * TAPS)
    reach = max(row_count, TAPS)

    def kernel(*refs):
        input_refs = refs[: len(inputs)]
        taps_ref, skip_ref, toeplitz_ref, out_ref, extended = refs[len(inputs) :]
        end = 0
        used = 0
        for term, (first, last) in zip(terms, spans, strict=True):
            total = input_refs[used][0, first:last].astype(jnp.float32)
            for ref in input_refs[used + 1 : used + len(term)]:
                total += ref[0, first:last].astype(jnp.float32)
            extended[end : end + last - first] = total.astype(jnp.bfloat16).astype(jnp.float32)
            used += len(term)
            end += last - first
        if row_count < TAPS:
            extended[end:] = jnp.zeros((TAPS - row_count, wide), jnp.float32)
        rows = TAPS + reach
        filtered = sum(
            taps_ref[lag : lag + 1] * extended[16 - lag : 16 - lag + rows] for lag in range(3)
        )
        product = filtered[:, width : 2 * width] * filtered[:, 2 * width :]
        product = product.astype(jnp.bfloat16)
        owner = lax.broadcasted_iota(jnp.int32, (2 * TAPS, width), 1) // GROUP
        for start in range(0, row_count, TAPS):
            start = min(start, reach - TAPS)
            size = min(TAPS, row_count)
            window = product[start : start + 2 * TAPS]
            spread = jnp.concatenate(
                [jnp.where(owner == f, window, jnp.zeros_like(window)) for f in range(filters)], 0
            )
            convolved = jnp.dot(toeplitz_ref[...], spread, preferred_element_type=jnp.float32)
            mixing = skip_ref[...] * window[TAPS:].astype(jnp.float32) + convolved
            queries = filtered[TAPS + start : 2 * TAPS + start, :width]
            out_ref[0, start : start + size] = (queries * mixing)[:size].astype(jnp.bfloat16)

    slot = lambda i: (i, 0, 0)
    fixed = lambda i: (0, 0)
    return pl.pallas_call(
        kernel,
        grid=(slots,),
        in_specs=[pl.BlockSpec((1,) + value.shape[1:], slot) for value in inputs]
        + [
            pl.BlockSpec((3, wide), fixed),
            pl.BlockSpec((1, width), fixed),
            pl.BlockSpec((TAPS, 2 * TAPS * filters), fixed),
        ],
        out_specs=pl.BlockSpec((1, row_count, width), slot),
        out_shape=jax.ShapeDtypeStruct((slots, row_count, width), jnp.bfloat16),
        scratch_shapes=[pltpu.VMEM((EDGE + reach, wide), jnp.float32)],
        compiler_params=pltpu.CompilerParams(vmem_limit_bytes=VMEM),
        cost_estimate=SHORT,
        name="gate",
    )(*inputs, short_taps, skip_gain, toeplitz)


def out_block(gating, w_out, block, count):
    rows, depth = gating.shape
    columns = w_out.shape[1] // count
    tile = min(columns, 512)
    steps = columns // tile

    def kernel(block_ref, gating_ref, w_ref, out_ref, held, sems):
        first = block_ref[0] * columns
        loads = []
        for i in range(steps):
            place = pl.ds(pl.multiple_of(first + i * tile, 128), tile)
            loads.append(pltpu.make_async_copy(w_ref.at[:, place], held.at[i], sems.at[i]))
        for load in loads:
            load.start()
        for i, load in enumerate(loads):
            load.wait()
            out_ref[:, i * tile : (i + 1) * tile] = jnp.dot(
                gating_ref[...], held[i], preferred_element_type=jnp.float32
            ).astype(jnp.bfloat16)

    vmem = pl.BlockSpec(memory_space=pltpu.VMEM)
    return pl.pallas_call(
        kernel,
        in_specs=[pl.BlockSpec(memory_space=pltpu.SMEM), vmem, pl.BlockSpec(memory_space=pl.ANY)],
        out_specs=vmem,
        out_shape=jax.ShapeDtypeStruct((rows, columns), jnp.bfloat16),
        scratch_shapes=[
            pltpu.VMEM((steps, depth, tile), jnp.bfloat16),
            pltpu.SemaphoreType.DMA((steps,)),
        ],
        compiler_params=pltpu.CompilerParams(vmem_limit_bytes=50 << 20),
        cost_estimate=SHORT,
        name="out_block",
    )(block.reshape(1).astype(jnp.int32), gating, w_out)


def toeplitz_of(medium_taps):
    cube_shape = (TAPS, TAPS, 2 * TAPS)
    lagged = (
        lax.broadcasted_iota(jnp.int32, cube_shape, 1)
        + TAPS
        - lax.broadcasted_iota(jnp.int32, cube_shape, 2)
    )
    onehot = (lagged == lax.broadcasted_iota(jnp.int32, cube_shape, 0)).astype(jnp.bfloat16)
    return jnp.einsum("jg,jis->igs", medium_taps.astype(jnp.bfloat16), onehot)


def row_parts(row_count, ranks):
    unit = 16 * ranks
    units = row_count // unit
    low = max(1, units // 4)
    middle = (units - low) // 2
    sizes = [size * unit for size in (units - low - middle, middle, low) if size]
    ends = [row_count - sum(sizes[:i]) for i in range(len(sizes))]
    return [(end - size, end) for end, size in zip(ends, sizes, strict=True)]


def per_device(tokens, norm_gain, w_in, short_taps, medium_taps, skip_gain, w_out):
    seq, ranks = lax.axis_size("seq"), lax.axis_size("chan")
    here, column = lax.axis_index("seq"), lax.axis_index("chan")
    near = seq // 4
    odd, layer = here % 2, here // 2
    half, place = layer // near, layer % near
    row_count = tokens.shape[0]
    depth = norm_gain.shape[0]
    channels = w_in.shape[2]
    mine = channels // near
    pieces = max(1, mine // 256)
    width = mine // pieces
    parts = row_parts(row_count, ranks)
    slab = w_in.shape[0] // 2
    order = jnp.stack(
        [(place ^ o) * 2 + (odd ^ p) for o in range(near) for p in range(2)]
    ).astype(jnp.int32)
    places = jnp.stack([column ^ i for i in range(ranks)]).astype(jnp.int32)
    state = {}

    def cut(i, o, h):
        if ("slab", h) not in state:
            rows = jnp.transpose(w_in[h * slab : (h + 1) * slab], (1, 0, 2))
            state["slab", h] = lax.optimization_barrier(rows)
        return lax.dynamic_slice_in_dim(state["slab", h], (place ^ o) * mine + i * width, width, 2)

    def near_w(i, h):
        if i < pieces:
            for o in range(1, near):
                state["w", i, o, 0, h] = swapped(cut(i, o, h), "seq", 2 * o)

    def pair_own_w(i, h):
        if i < pieces:
            state["w", i, 0, 0, h] = own = cut(i, 0, h)
            state["w", i, 0, 1, h] = swapped(own, "seq", 1)

    def pair_near_w(i, h):
        if i < pieces:
            for o in range(1, near):
                state["w", i, o, 1, h] = swapped(state["w", i, o, 0, h], "seq", 1)

    def share(first_part, last_part):
        for r in range(ranks):
            rows = []
            for first, last in parts[first_part:last_part]:
                size = (last - first) // ranks
                rows.append(lax.dynamic_slice_in_dim(tokens, first + (column ^ r) * size, size, 0))
            rows = jnp.concatenate(rows, 0)
            state["shared", first_part, r] = rows if r == 0 else swapped(rows, "chan", r)

    def norm(j):
        if j >= len(parts):
            return
        group = min(j, 1)
        start = (parts[group][1] - parts[j][1]) // ranks
        size = (parts[j][1] - parts[j][0]) // ranks
        widened = [
            state["shared", group, r][start : start + size].astype(jnp.float32) for r in range(ranks)
        ]
        square = sum(jnp.sum(piece * piece, axis=1, keepdims=True) for piece in widened)
        scale = lax.rsqrt(square / depth + EPSILON)
        gains = norm_gain.reshape(ranks, 1, depth // ranks)
        normed = jnp.stack(
            [
                (piece * scale * lax.dynamic_index_in_dim(gains, column ^ r, 0, False)).astype(jnp.bfloat16)
                for r, piece in enumerate(widened)
            ]
        )

        def of_half(which):
            chosen = [
                lax.dynamic_index_in_dim(normed, column ^ (which * (ranks // 2) + r), 0, False)
                for r in range(ranks // 2)
            ]
            return jnp.concatenate(chosen, 1)

        state["kept", j] = of_half(half)
        state["away", j] = of_half(1 - half)

    def cross(j):
        if j < len(parts):
            state["away", j] = swapped(state["away", j], "seq", 2 * near)

    def near_rows(kind, j):
        if j < len(parts):
            rows = state[kind, j]
            moved = [rows if o == 0 else swapped(rows, "seq", 2 * o) for o in range(near)]
            state[kind, j] = jnp.concatenate(moved, 0)

    def across(kind, j):
        if j < len(parts):
            rows = state[kind, j]
            moved = [rows if a == 0 else swapped(rows, "chan", 2 * a) for a in range(ranks // 2)]
            state[kind, j] = jnp.concatenate(moved, 0)

    def beside(kind, j):
        if j < len(parts):
            state["other", kind, j] = swapped(state[kind, j], "chan", 1)

    def multiplied(kind, i, j):
        rows = [state[kind, j], state["other", kind, j]]
        sections = [[state["w", i, o, p, h] for h in range(2)] for o in range(near) for p in range(2)]
        return project(order, places, rows, sections, near, ranks)

    def drop(*names):
        for key in [key for key in state if isinstance(key, tuple) and key[: len(names)] == names]:
            del state[key]

    def partial(i, j):
        if i < pieces and j < len(parts):
            state["partial", i, j] = multiplied("away", i, j)
            if i == pieces - 1:
                drop("away", j)
                drop("other", "away", j)

    def send(i, j):
        if i < pieces and j < len(parts):
            state["moved", i, j] = swapped(state.pop(("partial", i, j)), "seq", 2 * near)

    def own(i, j):
        if i < pieces and j < len(parts):
            state["own", i, j] = multiplied("kept", i, j)
            if i == pieces - 1:
                drop("kept", j)
                drop("other", "kept", j)

    def constants():
        short = lax.dynamic_slice_in_dim(short_taps, place * mine, mine, 2)
        skip = lax.dynamic_slice_in_dim(skip_gain, place * mine, mine, 0).reshape(1, mine)
        filters = medium_taps.shape[1] // near
        toeplitz = toeplitz_of(lax.dynamic_slice_in_dim(medium_taps, place * filters, filters, 1))
        some = filters // pieces
        for i in range(pieces):
            span = slice(i * width, (i + 1) * width)
            blocks = toeplitz[:, i * some : (i + 1) * some].reshape(TAPS, some * 2 * TAPS)
            state["constants", i, 0] = short[:, :, span].reshape(3, 3 * width)
            state["constants", i, 1] = skip[:, span]
            state["constants", i, 2] = blocks

    def step():
        held = lax.optimization_barrier(list(state.values()))
        state.update(zip(list(state), held, strict=True))

    share(0, 1)
    pair_own_w(0, 0)
    near_w(0, 0)
    step()
    norm(0)
    cross(0)
    share(1, len(parts))
    pair_own_w(0, 1)
    near_w(0, 1)
    step()
    for j in range(1, len(parts)):
        norm(j)
    drop("shared")
    cross(1)
    constants()
    near_rows("away", 0)
    pair_near_w(0, 0)
    step()
    cross(2)
    across("away", 0)
    near_rows("away", 1)
    pair_near_w(0, 1)
    step()
    beside("away", 0)
    partial(0, 0)
    across("away", 1)
    near_rows("away", 2)
    near_w(1, 0)
    pair_own_w(1, 0)
    step()
    send(0, 0)
    beside("away", 1)
    partial(0, 1)
    across("away", 2)
    near_w(1, 1)
    pair_own_w(1, 1)
    step()
    drop("slab")
    send(0, 1)
    beside("away", 2)
    partial(0, 2)
    near_rows("kept", 0)
    pair_near_w(1, 0)
    step()
    send(0, 2)
    across("kept", 0)
    near_rows("kept", 1)
    near_rows("kept", 2)
    pair_near_w(1, 1)
    step()
    partial(1, 0)
    send(1, 0)
    partial(1, 1)
    beside("kept", 0)
    across("kept", 1)
    own(0, 0)
    own(1, 0)
    step()
    far = [(2 * i + 1, 2 * (near + i)) for i in range(near)]

    def term(kind, i, j):
        value = state[kind, i, j]
        return value.reshape(near, value.shape[0] // near, 3 * width)

    def edges(i):
        edge = [term(kind, i, 0)[:, -EDGE:].astype(jnp.float32) for kind in ("own", "moved")]
        edge = (edge[0] + edge[1]).astype(jnp.bfloat16)
        edge = jnp.stack([lax.dynamic_index_in_dim(edge, place ^ o, 0, False) for o in range(near)])
        state["edge", i], state["other edge", i] = edge, swapped(edge, "seq", 1)

    def halo(i):
        edge, other = state.pop(("edge", i)), state.pop(("other edge", i))
        before = jnp.concatenate([lax.ppermute(edge[-1:], "seq", far), other[:-1]], 0)
        rows = jnp.where(odd == 1, other, before)
        rows = [lax.dynamic_index_in_dim(rows, place ^ o, 0, False) for o in range(near)]
        state["halo", i] = jnp.stack(rows)

    def passed_near(value):
        return [value[o] if o == 0 else swapped(value[o], "seq", 2 * o) for o in range(near)]

    last = len(parts) - 1

    def gated(i):
        terms = [(term("own", i, j), term("moved", i, j)) for j in reversed(range(len(parts)))]
        spans = [(0, EDGE)] + [(0, value.shape[1]) for value, _ in terms]
        constants = [state["constants", i, k] for k in range(3)]
        return gate([(state["halo", i],)] + terms, spans, row_count, *constants)

    def joined(gates):
        gating = jnp.zeros((row_count, channels), jnp.bfloat16)
        for o in range(near):
            shares = jnp.concatenate([piece[o] for piece in gates], 1)
            gating = lax.dynamic_update_slice(gating, shares, (0, (place ^ o) * mine))
        return gating

    def chip_sum(gating, a):
        target = column ^ (2 * a)
        other = swapped(out_block(gating, w_out, target ^ 1, ranks), "chan", 1)
        return out_block(gating, w_out, target, ranks).astype(jnp.float32) + other.astype(jnp.float32)

    def far_sums(gating):
        return [chip_sum(gating, a).astype(jnp.bfloat16) for a in range(1, ranks // 2)]

    send(1, 1)
    beside("kept", 1)
    across("kept", 2)
    partial(1, 2)
    own(0, 1)
    own(1, 1)
    for i in range(pieces):
        edges(i)
    step()
    send(1, 2)
    beside("kept", 2)
    for i in range(pieces):
        halo(i)
    if last > 1:
        own(0, last)
        own(1, last)
    drop("w")
    if pieces > 1:
        state["gated"] = passed_near(gated(0))
    step()
    gates = [state["gated"]] if pieces > 1 else []
    for i in range(len(gates), pieces):
        gates.append(passed_near(gated(i)))
    gating = joined(gates)
    state["gating"] = gating
    state["sums"] = far_sums(gating)
    state["block"] = out_block(gating, w_out, column ^ 1, ranks)
    step()
    received = [swapped(value, "chan", 2 * a) for a, value in enumerate(state["sums"], 1)]
    received.append(swapped(state["block"], "chan", 1))
    total = tokens.astype(jnp.float32)
    total += out_block(state["gating"], w_out, column, ranks).astype(jnp.float32)
    return (total + sum(value.astype(jnp.float32) for value in received)).astype(jnp.bfloat16)


def solution(mesh):
    in_specs = (
        P("seq", "chan"),
        P(),
        P("seq", None, "chan"),
        P(None, None, "chan"),
        P(None, "chan"),
        P("chan"),
        P("chan", None),
    )
    out_specs = P("seq", "chan")
    return jax.shard_map(
        per_device, mesh=mesh, in_specs=in_specs, out_specs=out_specs, check_vma=False
    )
```

```python
import jax
import jax.numpy as jnp
from jax import lax
from jax.experimental import pallas as pl
from jax.experimental.pallas import tpu as pltpu
from jax.sharding import PartitionSpec as P

TAPS = 128
GROUP = 16
EDGE = TAPS + 16
EPSILON = 1e-06
VMEM = 24 << 20
SHORT = pl.CostEstimate(flops=1, bytes_accessed=1, transcendentals=0)


def swapped(value, axis, bit):
    return lax.ppermute(value, axis, [(i, i ^ bit) for i in range(lax.axis_size(axis))])


def project(order, places, rows, sections, near, ranks):
    depth = rows[0].shape[1]
    slabs = len(sections[0])
    branches, slab, width = sections[0][0].shape
    step = slabs * slab
    each = 2 * rows[0].shape[0] // (ranks * near)
    span = ranks * each
    count = near * span
    wide = branches * width
    flat = [value for section in sections for value in section]

    def kernel(order_ref, places_ref, *refs):
        gathered, total = refs[-2:]
        out_ref = refs[-3]
        for i in range(ranks):
            place = pl.multiple_of(places_ref[i] * each, each)
            for o in range(near):
                start = ((i // 2) * near + o) * each
                gathered[pl.ds(o * span + place, each)] = refs[i % 2][start : start + each]
        for i in range(len(flat)):
            place = pl.multiple_of(order_ref[i // slabs] * step + (i % slabs) * slab, slab)
            part = gathered[:, pl.ds(place, slab)]
            for b in range(branches):
                columns = slice(b * width, (b + 1) * width)
                value = jnp.dot(part, refs[2 + i][b], preferred_element_type=jnp.float32)
                if i:
                    value += total[:, columns]
                if i < len(flat) - 1:
                    total[:, columns] = value
                else:
                    out_ref[:, columns] = value.astype(jnp.bfloat16)

    smem = pl.BlockSpec(memory_space=pltpu.SMEM)
    vmem = pl.BlockSpec(memory_space=pltpu.VMEM)
    return pl.pallas_call(
        kernel,
        in_specs=[smem, smem] + [vmem] * (2 + len(flat)),
        out_specs=vmem,
        out_shape=jax.ShapeDtypeStruct((count, wide), jnp.bfloat16),
        scratch_shapes=[
            pltpu.VMEM((count, depth), jnp.bfloat16),
            pltpu.VMEM((count, wide), jnp.float32),
        ],
        compiler_params=pltpu.CompilerParams(vmem_limit_bytes=VMEM),
        cost_estimate=SHORT,
        name="project",
    )(order, places, *rows, *flat)


def gate(terms, spans, row_count, short_taps, skip_gain, toeplitz):
    inputs = [value for term in terms for value in term]
    slots, _, wide = inputs[0].shape
    width = wide // 3
    filters = toeplitz.shape[1] // (2 * TAPS)
    reach = max(row_count, TAPS)

    def kernel(*refs):
        input_refs = refs[: len(inputs)]
        taps_ref, skip_ref, toeplitz_ref, out_ref, extended = refs[len(inputs) :]
        end = 0
        used = 0
        for term, (first, last) in zip(terms, spans, strict=True):
            total = input_refs[used][0, first:last].astype(jnp.float32)
            for ref in input_refs[used + 1 : used + len(term)]:
                total += ref[0, first:last].astype(jnp.float32)
            extended[end : end + last - first] = total.astype(jnp.bfloat16).astype(jnp.float32)
            used += len(term)
            end += last - first
        if row_count < TAPS:
            extended[end:] = jnp.zeros((TAPS - row_count, wide), jnp.float32)
        rows = TAPS + reach
        filtered = sum(
            taps_ref[lag : lag + 1] * extended[16 - lag : 16 - lag + rows] for lag in range(3)
        )
        product = filtered[:, width : 2 * width] * filtered[:, 2 * width :]
        product = product.astype(jnp.bfloat16)
        owner = lax.broadcasted_iota(jnp.int32, (2 * TAPS, width), 1) // GROUP
        for start in range(0, row_count, TAPS):
            start = min(start, reach - TAPS)
            size = min(TAPS, row_count)
            window = product[start : start + 2 * TAPS]
            spread = jnp.concatenate(
                [jnp.where(owner == f, window, jnp.zeros_like(window)) for f in range(filters)], 0
            )
            convolved = jnp.dot(toeplitz_ref[...], spread, preferred_element_type=jnp.float32)
            mixing = skip_ref[...] * window[TAPS:].astype(jnp.float32) + convolved
            queries = filtered[TAPS + start : 2 * TAPS + start, :width]
            out_ref[0, start : start + size] = (queries * mixing)[:size].astype(jnp.bfloat16)

    slot = lambda i: (i, 0, 0)
    fixed = lambda i: (0, 0)
    return pl.pallas_call(
        kernel,
        grid=(slots,),
        in_specs=[pl.BlockSpec((1,) + value.shape[1:], slot) for value in inputs]
        + [
            pl.BlockSpec((3, wide), fixed),
            pl.BlockSpec((1, width), fixed),
            pl.BlockSpec((TAPS, 2 * TAPS * filters), fixed),
        ],
        out_specs=pl.BlockSpec((1, row_count, width), slot),
        out_shape=jax.ShapeDtypeStruct((slots, row_count, width), jnp.bfloat16),
        scratch_shapes=[pltpu.VMEM((EDGE + reach, wide), jnp.float32)],
        compiler_params=pltpu.CompilerParams(vmem_limit_bytes=VMEM),
        cost_estimate=SHORT,
        name="gate",
    )(*inputs, short_taps, skip_gain, toeplitz)


def out_block(gating, w_out, block, count):
    rows, depth = gating.shape
    columns = w_out.shape[1] // count
    tile = min(columns, 512)
    steps = columns // tile

    def kernel(block_ref, gating_ref, w_ref, out_ref, held, sems):
        first = block_ref[0] * columns
        loads = []
        for i in range(steps):
            place = pl.ds(pl.multiple_of(first + i * tile, 128), tile)
            loads.append(pltpu.make_async_copy(w_ref.at[:, place], held.at[i], sems.at[i]))
        for load in loads:
            load.start()
        for i, load in enumerate(loads):
            load.wait()
            out_ref[:, i * tile : (i + 1) * tile] = jnp.dot(
                gating_ref[...], held[i], preferred_element_type=jnp.float32
            ).astype(jnp.bfloat16)

    vmem = pl.BlockSpec(memory_space=pltpu.VMEM)
    return pl.pallas_call(
        kernel,
        in_specs=[pl.BlockSpec(memory_space=pltpu.SMEM), vmem, pl.BlockSpec(memory_space=pl.ANY)],
        out_specs=vmem,
        out_shape=jax.ShapeDtypeStruct((rows, columns), jnp.bfloat16),
        scratch_shapes=[
            pltpu.VMEM((steps, depth, tile), jnp.bfloat16),
            pltpu.SemaphoreType.DMA((steps,)),
        ],
        compiler_params=pltpu.CompilerParams(vmem_limit_bytes=50 << 20),
        cost_estimate=SHORT,
        name="out_block",
    )(block.reshape(1).astype(jnp.int32), gating, w_out)


def toeplitz_of(medium_taps):
    cube_shape = (TAPS, TAPS, 2 * TAPS)
    lagged = (
        lax.broadcasted_iota(jnp.int32, cube_shape, 1)
        + TAPS
        - lax.broadcasted_iota(jnp.int32, cube_shape, 2)
    )
    onehot = (lagged == lax.broadcasted_iota(jnp.int32, cube_shape, 0)).astype(jnp.bfloat16)
    return jnp.einsum("jg,jis->igs", medium_taps.astype(jnp.bfloat16), onehot)


def row_parts(row_count, ranks):
    unit = 16 * ranks
    units = row_count // unit
    low = max(1, units // 4)
    middle = (units - low) // 2
    sizes = [size * unit for size in (units - low - middle, middle, low) if size]
    ends = [row_count - sum(sizes[:i]) for i in range(len(sizes))]
    return [(end - size, end) for end, size in zip(ends, sizes, strict=True)]


def per_device(tokens, norm_gain, w_in, short_taps, medium_taps, skip_gain, w_out):
    seq, ranks = lax.axis_size("seq"), lax.axis_size("chan")
    here, column = lax.axis_index("seq"), lax.axis_index("chan")
    near = seq // 4
    odd, layer = here % 2, here // 2
    half, place = layer // near, layer % near
    row_count = tokens.shape[0]
    depth = norm_gain.shape[0]
    channels = w_in.shape[2]
    mine = channels // near
    pieces = max(1, mine // 256)
    width = mine // pieces
    parts = row_parts(row_count, ranks)
    slab = w_in.shape[0] // 2
    order = jnp.stack(
        [(place ^ o) * 2 + (odd ^ p) for o in range(near) for p in range(2)]
    ).astype(jnp.int32)
    places = jnp.stack([column ^ i for i in range(ranks)]).astype(jnp.int32)
    state = {}

    def cut(i, o, h):
        if ("slab", h) not in state:
            rows = jnp.transpose(w_in[h * slab : (h + 1) * slab], (1, 0, 2))
            state["slab", h] = lax.optimization_barrier(rows)
        return lax.dynamic_slice_in_dim(state["slab", h], (place ^ o) * mine + i * width, width, 2)

    def near_w(i, h):
        if i < pieces:
            for o in range(1, near):
                state["w", i, o, 0, h] = swapped(cut(i, o, h), "seq", 2 * o)

    def pair_own_w(i, h):
        if i < pieces:
            state["w", i, 0, 0, h] = own = cut(i, 0, h)
            state["w", i, 0, 1, h] = swapped(own, "seq", 1)

    def pair_near_w(i, h):
        if i < pieces:
            for o in range(1, near):
                state["w", i, o, 1, h] = swapped(state["w", i, o, 0, h], "seq", 1)

    def share(first_part, last_part):
        for r in range(ranks):
            rows = []
            for first, last in parts[first_part:last_part]:
                size = (last - first) // ranks
                rows.append(lax.dynamic_slice_in_dim(tokens, first + (column ^ r) * size, size, 0))
            rows = jnp.concatenate(rows, 0)
            state["shared", first_part, r] = rows if r == 0 else swapped(rows, "chan", r)

    def norm(j):
        if j >= len(parts):
            return
        group = min(j, 1)
        start = (parts[group][1] - parts[j][1]) // ranks
        size = (parts[j][1] - parts[j][0]) // ranks
        widened = [
            state["shared", group, r][start : start + size].astype(jnp.float32) for r in range(ranks)
        ]
        square = sum(jnp.sum(piece * piece, axis=1, keepdims=True) for piece in widened)
        scale = lax.rsqrt(square / depth + EPSILON)
        gains = norm_gain.reshape(ranks, 1, depth // ranks)
        normed = jnp.stack(
            [
                (piece * scale * lax.dynamic_index_in_dim(gains, column ^ r, 0, False)).astype(jnp.bfloat16)
                for r, piece in enumerate(widened)
            ]
        )

        def of_half(which):
            chosen = [
                lax.dynamic_index_in_dim(normed, column ^ (which * (ranks // 2) + r), 0, False)
                for r in range(ranks // 2)
            ]
            return jnp.concatenate(chosen, 1)

        state["kept", j] = of_half(half)
        state["away", j] = of_half(1 - half)

    def cross(j):
        if j < len(parts):
            state["away", j] = swapped(state["away", j], "seq", 2 * near)

    def near_rows(kind, j):
        if j < len(parts):
            rows = state[kind, j]
            moved = [rows if o == 0 else swapped(rows, "seq", 2 * o) for o in range(near)]
            state[kind, j] = jnp.concatenate(moved, 0)

    def across(kind, j):
        if j < len(parts):
            rows = state[kind, j]
            moved = [rows if a == 0 else swapped(rows, "chan", 2 * a) for a in range(ranks // 2)]
            state[kind, j] = jnp.concatenate(moved, 0)

    def beside(kind, j):
        if j < len(parts):
            state["other", kind, j] = swapped(state[kind, j], "chan", 1)

    def multiplied(kind, i, j):
        rows = [state[kind, j], state["other", kind, j]]
        sections = [[state["w", i, o, p, h] for h in range(2)] for o in range(near) for p in range(2)]
        return project(order, places, rows, sections, near, ranks)

    def drop(*names):
        for key in [key for key in state if isinstance(key, tuple) and key[: len(names)] == names]:
            del state[key]

    def partial(i, j):
        if i < pieces and j < len(parts):
            state["partial", i, j] = multiplied("away", i, j)
            if i == pieces - 1:
                drop("away", j)
                drop("other", "away", j)

    def send(i, j):
        if i < pieces and j < len(parts):
            state["moved", i, j] = swapped(state.pop(("partial", i, j)), "seq", 2 * near)

    def own(i, j):
        if i < pieces and j < len(parts):
            state["own", i, j] = multiplied("kept", i, j)
            if i == pieces - 1:
                drop("kept", j)
                drop("other", "kept", j)

    def constants():
        short = lax.dynamic_slice_in_dim(short_taps, place * mine, mine, 2)
        skip = lax.dynamic_slice_in_dim(skip_gain, place * mine, mine, 0).reshape(1, mine)
        filters = medium_taps.shape[1] // near
        toeplitz = toeplitz_of(lax.dynamic_slice_in_dim(medium_taps, place * filters, filters, 1))
        some = filters // pieces
        for i in range(pieces):
            span = slice(i * width, (i + 1) * width)
            blocks = toeplitz[:, i * some : (i + 1) * some].reshape(TAPS, some * 2 * TAPS)
            state["constants", i, 0] = short[:, :, span].reshape(3, 3 * width)
            state["constants", i, 1] = skip[:, span]
            state["constants", i, 2] = blocks

    def step():
        held = lax.optimization_barrier(list(state.values()))
        state.update(zip(list(state), held, strict=True))

    share(0, 1)
    pair_own_w(0, 0)
    near_w(0, 0)
    step()
    norm(0)
    cross(0)
    share(1, len(parts))
    pair_own_w(0, 1)
    near_w(0, 1)
    step()
    for j in range(1, len(parts)):
        norm(j)
    drop("shared")
    cross(1)
    constants()
    near_rows("away", 0)
    pair_near_w(0, 0)
    step()
    cross(2)
    across("away", 0)
    near_rows("away", 1)
    pair_near_w(0, 1)
    step()
    beside("away", 0)
    partial(0, 0)
    across("away", 1)
    near_rows("away", 2)
    near_w(1, 0)
    pair_own_w(1, 0)
    step()
    send(0, 0)
    beside("away", 1)
    partial(0, 1)
    across("away", 2)
    near_w(1, 1)
    pair_own_w(1, 1)
    step()
    drop("slab")
    send(0, 1)
    beside("away", 2)
    partial(0, 2)
    near_rows("kept", 0)
    pair_near_w(1, 0)
    step()
    send(0, 2)
    across("kept", 0)
    near_rows("kept", 1)
    near_rows("kept", 2)
    pair_near_w(1, 1)
    step()
    partial(1, 0)
    send(1, 0)
    partial(1, 1)
    beside("kept", 0)
    across("kept", 1)
    own(0, 0)
    own(1, 0)
    step()
    far = [(2 * i + 1, 2 * (near + i)) for i in range(near)]

    def term(kind, i, j):
        value = state[kind, i, j]
        return value.reshape(near, value.shape[0] // near, 3 * width)

    def edges(i):
        edge = [term(kind, i, 0)[:, -EDGE:].astype(jnp.float32) for kind in ("own", "moved")]
        edge = (edge[0] + edge[1]).astype(jnp.bfloat16)
        edge = jnp.stack([lax.dynamic_index_in_dim(edge, place ^ o, 0, False) for o in range(near)])
        state["edge", i], state["other edge", i] = edge, swapped(edge, "seq", 1)

    def halo(i):
        edge, other = state.pop(("edge", i)), state.pop(("other edge", i))
        if i % 2:
            crossed = lax.ppermute(other[-1:], "seq", [(2 * k, 2 * (near + k)) for k in range(near)])
        else:
            crossed = lax.ppermute(edge[-1:], "seq", far)
        before = jnp.concatenate([crossed, other[:-1]], 0)
        rows = jnp.where(odd == 1, other, before)
        rows = [lax.dynamic_index_in_dim(rows, place ^ o, 0, False) for o in range(near)]
        state["halo", i] = jnp.stack(rows)

    def passed_near(value):
        return [value[o] if o == 0 else swapped(value[o], "seq", 2 * o) for o in range(near)]

    last = len(parts) - 1

    def gated(i):
        terms = [(term("own", i, j), term("moved", i, j)) for j in reversed(range(len(parts)))]
        spans = [(0, EDGE)] + [(0, value.shape[1]) for value, _ in terms]
        constants = [state["constants", i, k] for k in range(3)]
        return gate([(state["halo", i],)] + terms, spans, row_count, *constants)

    def joined(gates):
        gating = jnp.zeros((row_count, channels), jnp.bfloat16)
        for o in range(near):
            shares = jnp.concatenate([piece[o] for piece in gates], 1)
            gating = lax.dynamic_update_slice(gating, shares, (0, (place ^ o) * mine))
        return gating

    def chip_sum(gating, a):
        target = column ^ (2 * a)
        other = swapped(out_block(gating, w_out, target ^ 1, ranks), "chan", 1)
        return out_block(gating, w_out, target, ranks).astype(jnp.float32) + other.astype(jnp.float32)

    def far_sums(gating):
        return [chip_sum(gating, a).astype(jnp.bfloat16) for a in range(1, ranks // 2)]

    send(1, 1)
    beside("kept", 1)
    across("kept", 2)
    partial(1, 2)
    own(0, 1)
    own(1, 1)
    for i in range(pieces):
        edges(i)
    step()
    send(1, 2)
    beside("kept", 2)
    for i in range(pieces):
        halo(i)
    if last > 1:
        own(0, last)
        own(1, last)
    drop("w")
    if pieces > 1:
        state["gated"] = passed_near(gated(0))
    step()
    gates = [state["gated"]] if pieces > 1 else []
    for i in range(len(gates), pieces):
        gates.append(passed_near(gated(i)))
    gating = joined(gates)
    state["gating"] = gating
    state["sums"] = far_sums(gating)
    state["block"] = out_block(gating, w_out, column ^ 1, ranks)
    step()
    received = [swapped(value, "chan", 2 * a) for a, value in enumerate(state["sums"], 1)]
    received.append(swapped(state["block"], "chan", 1))
    total = tokens.astype(jnp.float32)
    total += out_block(state["gating"], w_out, column, ranks).astype(jnp.float32)
    return (total + sum(value.astype(jnp.float32) for value in received)).astype(jnp.bfloat16)


def solution(mesh):
    in_specs = (
        P("seq", "chan"),
        P(),
        P("seq", None, "chan"),
        P(None, None, "chan"),
        P(None, "chan"),
        P("chan"),
        P("chan", None),
    )
    out_specs = P("seq", "chan")
    return jax.shard_map(
        per_device, mesh=mesh, in_specs=in_specs, out_specs=out_specs, check_vma=False
    )
```

```python
import jax
import jax.numpy as jnp
from jax import lax
from jax.experimental import pallas as pl
from jax.experimental.pallas import tpu as pltpu
from jax.sharding import PartitionSpec as P

TAPS = 128
GROUP = 16
EDGE = TAPS + 16
EPSILON = 1e-06
VMEM = 24 << 20
SHORT = pl.CostEstimate(flops=1, bytes_accessed=1, transcendentals=0)


def swapped(value, axis, bit):
    return lax.ppermute(value, axis, [(i, i ^ bit) for i in range(lax.axis_size(axis))])


def project(order, places, rows, sections, near, ranks):
    depth = rows[0].shape[1]
    slabs = len(sections[0])
    branches, slab, width = sections[0][0].shape
    step = slabs * slab
    each = 2 * rows[0].shape[0] // (ranks * near)
    span = ranks * each
    count = near * span
    wide = branches * width
    flat = [value for section in sections for value in section]

    def kernel(order_ref, places_ref, *refs):
        gathered, total = refs[-2:]
        out_ref = refs[-3]
        for i in range(ranks):
            place = pl.multiple_of(places_ref[i] * each, each)
            for o in range(near):
                start = ((i // 2) * near + o) * each
                gathered[pl.ds(o * span + place, each)] = refs[i % 2][start : start + each]
        for i in range(len(flat)):
            place = pl.multiple_of(order_ref[i // slabs] * step + (i % slabs) * slab, slab)
            part = gathered[:, pl.ds(place, slab)]
            for b in range(branches):
                columns = slice(b * width, (b + 1) * width)
                value = jnp.dot(part, refs[2 + i][b], preferred_element_type=jnp.float32)
                if i:
                    value += total[:, columns]
                if i < len(flat) - 1:
                    total[:, columns] = value
                else:
                    out_ref[:, columns] = value.astype(jnp.bfloat16)

    smem = pl.BlockSpec(memory_space=pltpu.SMEM)
    vmem = pl.BlockSpec(memory_space=pltpu.VMEM)
    return pl.pallas_call(
        kernel,
        in_specs=[smem, smem] + [vmem] * (2 + len(flat)),
        out_specs=vmem,
        out_shape=jax.ShapeDtypeStruct((count, wide), jnp.bfloat16),
        scratch_shapes=[
            pltpu.VMEM((count, depth), jnp.bfloat16),
            pltpu.VMEM((count, wide), jnp.float32),
        ],
        compiler_params=pltpu.CompilerParams(vmem_limit_bytes=VMEM),
        cost_estimate=SHORT,
        name="project",
    )(order, places, *rows, *flat)


def gate(terms, spans, row_count, short_taps, skip_gain, toeplitz):
    inputs = [value for term in terms for value in term]
    slots, _, wide = inputs[0].shape
    width = wide // 3
    filters = toeplitz.shape[1] // (2 * TAPS)
    reach = max(row_count, TAPS)

    def kernel(*refs):
        input_refs = refs[: len(inputs)]
        taps_ref, skip_ref, toeplitz_ref, out_ref, extended = refs[len(inputs) :]
        end = 0
        used = 0
        for term, (first, last) in zip(terms, spans, strict=True):
            total = input_refs[used][0, first:last].astype(jnp.float32)
            for ref in input_refs[used + 1 : used + len(term)]:
                total += ref[0, first:last].astype(jnp.float32)
            extended[end : end + last - first] = total.astype(jnp.bfloat16).astype(jnp.float32)
            used += len(term)
            end += last - first
        if row_count < TAPS:
            extended[end:] = jnp.zeros((TAPS - row_count, wide), jnp.float32)
        rows = TAPS + reach
        filtered = sum(
            taps_ref[lag : lag + 1] * extended[16 - lag : 16 - lag + rows] for lag in range(3)
        )
        product = filtered[:, width : 2 * width] * filtered[:, 2 * width :]
        product = product.astype(jnp.bfloat16)
        owner = lax.broadcasted_iota(jnp.int32, (2 * TAPS, width), 1) // GROUP
        for start in range(0, row_count, TAPS):
            start = min(start, reach - TAPS)
            size = min(TAPS, row_count)
            window = product[start : start + 2 * TAPS]
            spread = jnp.concatenate(
                [jnp.where(owner == f, window, jnp.zeros_like(window)) for f in range(filters)], 0
            )
            convolved = jnp.dot(toeplitz_ref[...], spread, preferred_element_type=jnp.float32)
            mixing = skip_ref[...] * window[TAPS:].astype(jnp.float32) + convolved
            queries = filtered[TAPS + start : 2 * TAPS + start, :width]
            out_ref[0, start : start + size] = (queries * mixing)[:size].astype(jnp.bfloat16)

    slot = lambda i: (i, 0, 0)
    fixed = lambda i: (0, 0)
    return pl.pallas_call(
        kernel,
        grid=(slots,),
        in_specs=[pl.BlockSpec((1,) + value.shape[1:], slot) for value in inputs]
        + [
            pl.BlockSpec((3, wide), fixed),
            pl.BlockSpec((1, width), fixed),
            pl.BlockSpec((TAPS, 2 * TAPS * filters), fixed),
        ],
        out_specs=pl.BlockSpec((1, row_count, width), slot),
        out_shape=jax.ShapeDtypeStruct((slots, row_count, width), jnp.bfloat16),
        scratch_shapes=[pltpu.VMEM((EDGE + reach, wide), jnp.float32)],
        compiler_params=pltpu.CompilerParams(vmem_limit_bytes=VMEM),
        cost_estimate=SHORT,
        name="gate",
    )(*inputs, short_taps, skip_gain, toeplitz)


def out_block(gating, w_out, block, count):
    rows, depth = gating.shape
    columns = w_out.shape[1] // count
    tile = min(columns, 512)
    steps = columns // tile

    def kernel(block_ref, gating_ref, w_ref, out_ref, held, sems):
        first = block_ref[0] * columns
        loads = []
        for i in range(steps):
            place = pl.ds(pl.multiple_of(first + i * tile, 128), tile)
            loads.append(pltpu.make_async_copy(w_ref.at[:, place], held.at[i], sems.at[i]))
        for load in loads:
            load.start()
        for i, load in enumerate(loads):
            load.wait()
            out_ref[:, i * tile : (i + 1) * tile] = jnp.dot(
                gating_ref[...], held[i], preferred_element_type=jnp.float32
            ).astype(jnp.bfloat16)

    vmem = pl.BlockSpec(memory_space=pltpu.VMEM)
    return pl.pallas_call(
        kernel,
        in_specs=[pl.BlockSpec(memory_space=pltpu.SMEM), vmem, pl.BlockSpec(memory_space=pl.ANY)],
        out_specs=vmem,
        out_shape=jax.ShapeDtypeStruct((rows, columns), jnp.bfloat16),
        scratch_shapes=[
            pltpu.VMEM((steps, depth, tile), jnp.bfloat16),
            pltpu.SemaphoreType.DMA((steps,)),
        ],
        compiler_params=pltpu.CompilerParams(vmem_limit_bytes=50 << 20),
        cost_estimate=SHORT,
        name="out_block",
    )(block.reshape(1).astype(jnp.int32), gating, w_out)


def toeplitz_of(medium_taps):
    cube_shape = (TAPS, TAPS, 2 * TAPS)
    lagged = (
        lax.broadcasted_iota(jnp.int32, cube_shape, 1)
        + TAPS
        - lax.broadcasted_iota(jnp.int32, cube_shape, 2)
    )
    onehot = (lagged == lax.broadcasted_iota(jnp.int32, cube_shape, 0)).astype(jnp.bfloat16)
    return jnp.einsum("jg,jis->igs", medium_taps.astype(jnp.bfloat16), onehot)


def row_parts(row_count, ranks):
    unit = 16 * ranks
    units = row_count // unit
    low = max(1, units // 4)
    middle = (units - low) // 2
    sizes = [size * unit for size in (units - low - middle, middle, low) if size]
    ends = [row_count - sum(sizes[:i]) for i in range(len(sizes))]
    return [(end - size, end) for end, size in zip(ends, sizes, strict=True)]


def per_device(tokens, norm_gain, w_in, short_taps, medium_taps, skip_gain, w_out):
    seq, ranks = lax.axis_size("seq"), lax.axis_size("chan")
    here, column = lax.axis_index("seq"), lax.axis_index("chan")
    near = seq // 4
    odd, layer = here % 2, here // 2
    half, place = layer // near, layer % near
    row_count = tokens.shape[0]
    depth = norm_gain.shape[0]
    channels = w_in.shape[2]
    mine = channels // near
    pieces = max(1, mine // 256)
    width = mine // pieces
    parts = row_parts(row_count, ranks)
    slab = w_in.shape[0] // 2
    order = jnp.stack(
        [(place ^ o) * 2 + (odd ^ p) for o in range(near) for p in range(2)]
    ).astype(jnp.int32)
    places = jnp.stack([column ^ i for i in range(ranks)]).astype(jnp.int32)
    state = {}

    def cut(i, o, h):
        if ("slab", h) not in state:
            rows = jnp.transpose(w_in[h * slab : (h + 1) * slab], (1, 0, 2))
            state["slab", h] = lax.optimization_barrier(rows)
        return lax.dynamic_slice_in_dim(state["slab", h], (place ^ o) * mine + i * width, width, 2)

    def near_w(i, h):
        if i < pieces:
            for o in range(1, near):
                state["w", i, o, 0, h] = swapped(cut(i, o, h), "seq", 2 * o)

    def pair_own_w(i, h):
        if i < pieces:
            state["w", i, 0, 0, h] = own = cut(i, 0, h)
            state["w", i, 0, 1, h] = swapped(own, "seq", 1)

    def pair_near_w(i, h):
        if i < pieces:
            for o in range(1, near):
                state["w", i, o, 1, h] = swapped(state["w", i, o, 0, h], "seq", 1)

    def share(first_part, last_part):
        for r in range(ranks):
            rows = []
            for first, last in parts[first_part:last_part]:
                size = (last - first) // ranks
                rows.append(lax.dynamic_slice_in_dim(tokens, first + (column ^ r) * size, size, 0))
            rows = jnp.concatenate(rows, 0)
            state["shared", first_part, r] = rows if r == 0 else swapped(rows, "chan", r)

    def norm(j):
        if j >= len(parts):
            return
        group = min(j, 1)
        start = (parts[group][1] - parts[j][1]) // ranks
        size = (parts[j][1] - parts[j][0]) // ranks
        widened = [
            state["shared", group, r][start : start + size].astype(jnp.float32) for r in range(ranks)
        ]
        square = sum(jnp.sum(piece * piece, axis=1, keepdims=True) for piece in widened)
        scale = lax.rsqrt(square / depth + EPSILON)
        gains = norm_gain.reshape(ranks, 1, depth // ranks)
        normed = jnp.stack(
            [
                (piece * scale * lax.dynamic_index_in_dim(gains, column ^ r, 0, False)).astype(jnp.bfloat16)
                for r, piece in enumerate(widened)
            ]
        )

        def of_half(which):
            chosen = [
                lax.dynamic_index_in_dim(normed, column ^ (which * (ranks // 2) + r), 0, False)
                for r in range(ranks // 2)
            ]
            return jnp.concatenate(chosen, 1)

        state["kept", j] = of_half(half)
        state["away", j] = of_half(1 - half)

    def cross(j):
        if j < len(parts):
            state["away", j] = swapped(state["away", j], "seq", 2 * near)

    def near_rows(kind, j):
        if j < len(parts):
            rows = state[kind, j]
            moved = [rows if o == 0 else swapped(rows, "seq", 2 * o) for o in range(near)]
            state[kind, j] = jnp.concatenate(moved, 0)

    def across(kind, j):
        if j < len(parts):
            rows = state[kind, j]
            moved = [rows if a == 0 else swapped(rows, "chan", 2 * a) for a in range(ranks // 2)]
            state[kind, j] = jnp.concatenate(moved, 0)

    def beside(kind, j):
        if j < len(parts):
            state["other", kind, j] = swapped(state[kind, j], "chan", 1)

    def multiplied(kind, i, j):
        rows = [state[kind, j], state["other", kind, j]]
        sections = [[state["w", i, o, p, h] for h in range(2)] for o in range(near) for p in range(2)]
        return project(order, places, rows, sections, near, ranks)

    def drop(*names):
        for key in [key for key in state if isinstance(key, tuple) and key[: len(names)] == names]:
            del state[key]

    def partial(i, j):
        if i < pieces and j < len(parts):
            state["partial", i, j] = multiplied("away", i, j)
            if i == pieces - 1:
                drop("away", j)
                drop("other", "away", j)

    def send(i, j):
        if i < pieces and j < len(parts):
            state["moved", i, j] = swapped(state.pop(("partial", i, j)), "seq", 2 * near)

    def own(i, j):
        if i < pieces and j < len(parts):
            state["own", i, j] = multiplied("kept", i, j)
            if i == pieces - 1:
                drop("kept", j)
                drop("other", "kept", j)

    def constants():
        short = lax.dynamic_slice_in_dim(short_taps, place * mine, mine, 2)
        skip = lax.dynamic_slice_in_dim(skip_gain, place * mine, mine, 0).reshape(1, mine)
        filters = medium_taps.shape[1] // near
        toeplitz = toeplitz_of(lax.dynamic_slice_in_dim(medium_taps, place * filters, filters, 1))
        some = filters // pieces
        for i in range(pieces):
            span = slice(i * width, (i + 1) * width)
            blocks = toeplitz[:, i * some : (i + 1) * some].reshape(TAPS, some * 2 * TAPS)
            state["constants", i, 0] = short[:, :, span].reshape(3, 3 * width)
            state["constants", i, 1] = skip[:, span]
            state["constants", i, 2] = blocks

    def step():
        held = lax.optimization_barrier(list(state.values()))
        state.update(zip(list(state), held, strict=True))

    share(0, 1)
    pair_own_w(0, 0)
    near_w(0, 0)
    step()
    norm(0)
    cross(0)
    share(1, len(parts))
    pair_own_w(0, 1)
    near_w(0, 1)
    step()
    for j in range(1, len(parts)):
        norm(j)
    drop("shared")
    cross(1)
    constants()
    near_rows("away", 0)
    pair_near_w(0, 0)
    step()
    cross(2)
    across("away", 0)
    near_rows("away", 1)
    pair_near_w(0, 1)
    step()
    beside("away", 0)
    partial(0, 0)
    across("away", 1)
    near_rows("away", 2)
    near_w(1, 0)
    pair_own_w(1, 0)
    step()
    send(0, 0)
    beside("away", 1)
    partial(0, 1)
    across("away", 2)
    near_w(1, 1)
    pair_own_w(1, 1)
    step()
    drop("slab")
    send(0, 1)
    beside("away", 2)
    partial(0, 2)
    near_rows("kept", 0)
    pair_near_w(1, 0)
    step()
    send(0, 2)
    across("kept", 0)
    near_rows("kept", 1)
    pair_near_w(1, 1)
    step()
    partial(1, 0)
    send(1, 0)
    partial(1, 1)
    beside("kept", 0)
    across("kept", 1)
    near_rows("kept", 2)
    own(0, 0)
    own(1, 0)
    step()

    def term(kind, i, j):
        value = state[kind, i, j]
        return value.reshape(near, value.shape[0] // near, 3 * width)

    def edges(i):
        edge = [term(kind, i, 0)[:, -EDGE:].astype(jnp.float32) for kind in ("own", "moved")]
        edge = (edge[0] + edge[1]).astype(jnp.bfloat16)
        edge = jnp.stack([lax.dynamic_index_in_dim(edge, place ^ o, 0, False) for o in range(near)])
        state["edge", i], state["other edge", i] = edge, swapped(edge, "seq", 1)

    def halo(i):
        edge, other = state.pop(("edge", i)), state.pop(("other edge", i))
        pairs = [
            ((2 * k + 1 - c % 2) * ranks + c, 2 * (near + k) * ranks + c)
            for k in range(near)
            for c in range(ranks)
        ]
        leaving = jnp.where(odd == 1, edge[-1], other[-1])
        packed = jnp.concatenate([leaving[:, width : 2 * width], leaving[:, 2 * width :], leaving[-16:, :width]], 0)
        packed = lax.ppermute(packed, ("seq", "chan"), pairs)
        first = jnp.concatenate([jnp.zeros((EDGE - 16, width), jnp.bfloat16), packed[2 * EDGE :]], 0)
        crossed = jnp.concatenate([first, packed[:EDGE], packed[EDGE : 2 * EDGE]], 1)[None]
        before = jnp.concatenate([crossed, other[:-1]], 0)
        rows = jnp.where(odd == 1, other, before)
        rows = [lax.dynamic_index_in_dim(rows, place ^ o, 0, False) for o in range(near)]
        state["halo", i] = jnp.stack(rows)

    def passed_near(value):
        return [value[o] if o == 0 else swapped(value[o], "seq", 2 * o) for o in range(near)]

    last = len(parts) - 1

    def gated(i):
        terms = [(term("own", i, j), term("moved", i, j)) for j in reversed(range(len(parts)))]
        spans = [(0, EDGE)] + [(0, value.shape[1]) for value, _ in terms]
        constants = [state["constants", i, k] for k in range(3)]
        return gate([(state["halo", i],)] + terms, spans, row_count, *constants)

    def joined(gates):
        gating = jnp.zeros((row_count, channels), jnp.bfloat16)
        for o in range(near):
            shares = jnp.concatenate([piece[o] for piece in gates], 1)
            gating = lax.dynamic_update_slice(gating, shares, (0, (place ^ o) * mine))
        return gating

    def chip_sum(gating, a):
        target = column ^ (2 * a)
        other = swapped(out_block(gating, w_out, target ^ 1, ranks), "chan", 1)
        return out_block(gating, w_out, target, ranks).astype(jnp.float32) + other.astype(jnp.float32)

    def far_sums(gating):
        return [chip_sum(gating, a).astype(jnp.bfloat16) for a in range(1, ranks // 2)]

    send(1, 1)
    beside("kept", 1)
    across("kept", 2)
    partial(1, 2)
    own(0, 1)
    own(1, 1)
    for i in range(pieces):
        edges(i)
    step()
    send(1, 2)
    beside("kept", 2)
    for i in range(pieces):
        halo(i)
    if last > 1:
        own(0, last)
        own(1, last)
    drop("w")
    if pieces > 1:
        state["gated"] = passed_near(gated(0))
    step()
    gates = [state["gated"]] if pieces > 1 else []
    for i in range(len(gates), pieces):
        gates.append(passed_near(gated(i)))
    gating = joined(gates)
    state["gating"] = gating
    state["sums"] = far_sums(gating)
    state["block"] = out_block(gating, w_out, column ^ 1, ranks)
    step()
    received = [swapped(value, "chan", 2 * a) for a, value in enumerate(state["sums"], 1)]
    received.append(swapped(state["block"], "chan", 1))
    total = tokens.astype(jnp.float32)
    total += out_block(state["gating"], w_out, column, ranks).astype(jnp.float32)
    return (total + sum(value.astype(jnp.float32) for value in received)).astype(jnp.bfloat16)


def solution(mesh):
    in_specs = (
        P("seq", "chan"),
        P(),
        P("seq", None, "chan"),
        P(None, None, "chan"),
        P(None, "chan"),
        P("chan"),
        P("chan", None),
    )
    out_specs = P("seq", "chan")
    return jax.shard_map(
        per_device, mesh=mesh, in_specs=in_specs, out_specs=out_specs, check_vma=False
    )
```
